1024 devices in a mesh: space: 256 (over x, z, core), band: 4 (over y).
Axes of the slice: x: 4, y: 4, z: 32, core: 2. Of those that a mesh axis runs over, the one named last changes fastest.
Arguments:
- wave_in: bfloat16 [4096, 16, 16, 512], P('space', None, None, 'band'), parts along dimension 3, may hold values from -6 to 6
- mass_scale: float32 [4096, 256], P('space'), may hold values from 0.5 to 1
- potential: float32 [4096, 256], P('space'), may hold values from -2 to 1
- elem_scale: float32 [512, 2, 2], P('space'), may hold values from 0.5 to 1.5
- stiffness: bfloat16 [729, 729], replicated, as said below
- proj_lower: bfloat16 [256, 729, 32], P('space'), may hold values from -0.21875 to 0.21875
- proj_upper: bfloat16 [256, 729, 32], P('space'), may hold values from -0.21875 to 0.21875
- kb_coef: float32 [256, 32], P('space'), may hold values from -3 to 3
- atom_column: int32 [256], P('space'), may hold values from 0 to 3
- chan_count: int32 [256], P('space'), may hold values from 8 to 32
- upper_column: int32 [256], P('space'), may hold values from 0 to 3
Outputs:
- filtered: bfloat16 [4096, 16, 16, 512], P('space', None, None, 'band'), parts along dimension 3
- coefficients: float32 [256, 32, 512], P('space', None, 'band'), parts along dimension 2
The draws below stay inside these ranges and needn't reach their ends.
There are 4 independent parts, one for each index of `band`. The reference program is written for one: setup_inputs(seed, part) draws one part's arguments, and reference() takes and returns one part's arrays. A program takes and returns all parts, laid end to end along the dimension named above; an argument that names none is the same for every part. Nothing has to cross between parts.
Inputs may be any that keep to these rules, and one draw needn't show every extreme that they name: stiffness is symmetric.
All inputs are finite; a program needn't handle non-finite values.
Results may differ from the reference program's by a relative error of at most 0.006.
Values may be sent and summed in bfloat16 or wider, within the bound.
A program may use at most 32 MiB of HBM per device.

```python
import math
import jax
import jax.numpy as jnp
from jax import lax

ORDER = 8
CH = 32
NB = 128
ATOM_DEV = 1
CS = 16
ELN = 729
NZ = 4096
EZ = 512
ATOMS = 256
N_SPACE = 256


def draw_stiffness(key, part):
    off_key, diag_key = jax.random.split(jax.random.fold_in(key, 17))
    spread = 0.5 / ELN ** 0.5
    off_diagonal = jnp.clip(jax.random.normal(off_key, (ELN, ELN), jnp.float32) * spread, -4.0 * spread, 4.0 * spread)
    symmetric = 0.5 * (off_diagonal + off_diagonal.T)
    diagonal = jax.random.uniform(diag_key, (ELN,), jnp.float32, 0.5, 1.0)
    return (symmetric + jnp.diag(diagonal)).astype(jnp.bfloat16)


def plant(result, own_key, least, high):
    spot = [jax.random.randint(jax.random.fold_in(own_key, axis), (), 0, length) for axis, length in enumerate(result.shape)]
    main_axis = result.shape.index(max(result.shape))
    next_to = spot[:main_axis] + [(spot[main_axis] + 1) % result.shape[main_axis]] + spot[main_axis + 1:]
    return result.at[tuple(spot)].set(least).at[tuple(next_to)].set(high)


def block_levels(rng, dims, cuts, low, top_value):
    def one(axis_at, parts):
        steps = jax.random.uniform(jax.random.fold_in(jax.random.fold_in(rng, 6), axis_at), (parts,), jnp.float32, low / len(cuts), top_value / len(cuts))
        return jnp.repeat(jnp.exp(steps), dims[axis_at] // parts).reshape((-1,) + (1,) * (len(dims) - axis_at - 1))

    factor_of = one(*cuts[0])
    for cut in cuts[1:]:
        factor_of = factor_of * one(*cut)
    return factor_of


def gaussian(stream_key, shape, width, limit, shards=(), kind=jnp.bfloat16):
    result = width * jax.random.normal(stream_key, shape, jnp.float32)
    if shards:
        result = result * block_levels(stream_key, shape, shards, -0.22, 0.18)
    return jnp.clip(result, -limit, limit).astype(kind)


def setup_inputs(seed: int = 0, part: int = 0) -> dict:
    key_of = jax.random.split(jax.random.key(seed), 12)
    part_keys = jax.random.split(jax.random.fold_in(key_of[11], part), 12)
    wave_in = gaussian(part_keys[0], (NZ, CS, CS, NB), 1.0, 6.0, ((0, 256),))
    mass_scale = jnp.clip(jnp.exp(math.log(1.0) - 0.6931472 * jax.random.uniform(key_of[1], (NZ, CS * CS), jnp.float32) ** block_levels(key_of[1], (NZ, CS * CS), ((0, 256),), -0.2, 0.2)), 0.5, 1.0)
    potential = jnp.clip(-2.0 + 3.0 * jax.random.uniform(key_of[2], (NZ, CS * CS), jnp.float32) ** block_levels(key_of[2], (NZ, CS * CS), ((0, 256),), -0.2, 0.2), -2.0, 1.0)
    elem_scale = jnp.clip(jnp.exp(math.log(1.5) - 1.0986123 * jax.random.uniform(key_of[3], (EZ, 2, 2), jnp.float32) ** block_levels(key_of[3], (EZ, 2, 2), ((0, 256),), -0.2, 0.2)), 0.5, 1.5)
    stiffness = draw_stiffness(jax.random.fold_in(key_of[11], 71), part)
    proj_lower = gaussian(key_of[5], (ATOMS, ELN, CH), ELN ** -0.5, 0.21875, ((0, 256),))
    proj_upper = gaussian(key_of[6], (ATOMS, ELN, CH), ELN ** -0.5, 0.21875, ((0, 256),))
    kb_coef = jnp.clip(jax.random.uniform(key_of[7], (ATOMS, CH), jnp.float32, -3.0, 3.0) * block_levels(key_of[7], (ATOMS, CH), ((0, 256),), -0.4, 0.0), -3.0, 3.0)
    atom_column = plant(jax.random.randint(key_of[8], (ATOMS,), 0, 4), jax.random.fold_in(key_of[8], 1), 0, 3).astype(jnp.int32)
    chan_count = plant(jax.random.randint(key_of[9], (ATOMS,), CH // 4, CH + 1), jax.random.fold_in(key_of[9], 1), CH // 4, CH).astype(jnp.int32)
    upper_column = plant(jax.random.randint(key_of[10], (ATOMS,), 0, 4), jax.random.fold_in(key_of[10], 1), 0, 3).astype(jnp.int32)
    return dict(wave_in=wave_in, mass_scale=mass_scale, potential=potential, elem_scale=elem_scale, stiffness=stiffness, proj_lower=proj_lower, proj_upper=proj_upper, kb_coef=kb_coef, atom_column=atom_column, chan_count=chan_count, upper_column=upper_column)


spectrum_center = 1.0
spectrum_half = 6.0
highest = lax.Precision.HIGHEST


def wrap_sides(planes):
    planes = jnp.concatenate([planes, planes[:, :1]], axis=1)
    return jnp.concatenate([planes, planes[:, :, :1]], axis=2)


def layer_blocks(layer_nodes, degree):
    points = degree + 1
    gathered = []
    for across in range(2):
        for column in range(2):
            portion = layer_nodes[:, across * degree:across * degree + points, column * degree:column * degree + points]
            gathered.append(portion.reshape(points * points * points, layer_nodes.shape[-1]))
    return jnp.stack(gathered)


def assemble_blocks(results, degree):
    points = degree + 1
    extent = 2 * degree + 1
    band_count = results.shape[-1]
    summed = jnp.zeros((extent, extent, extent, band_count), jnp.float32)
    number = 0
    for height in range(2):
        for across in range(2):
            for column in range(2):
                summed = summed.at[height * degree:height * degree + points, across * degree:across * degree + points, column * degree:column * degree + points].add(results[number].reshape(points, points, points, band_count))
                number = number + 1
    summed = summed[:, :, :-1].at[:, :, 0].add(summed[:, :, -1])
    summed = summed[:, :-1].at[:, 0].add(summed[:, -1])
    return summed


def split_slab(slab_nodes, next_plane, degree):
    bottom_blocks = layer_blocks(wrap_sides(slab_nodes[:degree + 1]), degree)
    top_blocks = layer_blocks(wrap_sides(jnp.concatenate([slab_nodes[degree:], next_plane[None]], axis=0)), degree)
    return bottom_blocks, top_blocks


def project_ref(projector, blocks, columns):
    chosen = jnp.take(blocks, columns, axis=0)
    return jnp.einsum("anc,anb->acb", projector.astype(jnp.float32), chosen.astype(jnp.float32), precision=highest)


def scatter_ref(projector, coef_block, columns):
    values = jnp.einsum("anc,acb->anb", projector.astype(jnp.float32), coef_block.astype(jnp.float32), precision=highest)
    onehot = (columns[:, None] == jnp.arange(4, dtype=jnp.int32)[None, :]).astype(jnp.float32)
    return jnp.einsum("ak,anb->knb", onehot, values, precision=highest)


def coefficient_sums(nodal_field, lower_slabs, upper_slabs, own_columns, upper_columns, degree):
    next_planes = jnp.roll(nodal_field[:, 0], -1, axis=0)

    def one_slab(slab_items):
        slab_nodes, next_plane, lower_proj, upper_proj, lower_cols, upper_cols = slab_items
        bottom_blocks, top_blocks = split_slab(slab_nodes, next_plane, degree)
        return project_ref(upper_proj, bottom_blocks, upper_cols), project_ref(lower_proj, top_blocks, lower_cols)

    held_part, own_part = lax.map(one_slab, (nodal_field, next_planes, lower_slabs, upper_slabs, own_columns, upper_columns))
    return own_part + jnp.roll(held_part, -1, axis=0)


def operator_ref(nodal_field, stiffness, scales, mass_nodes, local_potential, lower_slabs, upper_slabs, weights, own_columns, upper_columns, degree):
    coef_total = coefficient_sums(nodal_field, lower_slabs, upper_slabs, own_columns, upper_columns, degree)
    scaled = (coef_total * weights[..., None]).astype(jnp.bfloat16)
    below_scaled = jnp.roll(scaled, 1, axis=0)
    next_planes = jnp.roll(nodal_field[:, 0], -1, axis=0)
    stiff_f32 = stiffness.astype(jnp.float32)

    def one_slab(slab_items):
        slab_nodes, next_plane, slab_scale, lower_proj, upper_proj, own_coef, below_coef, lower_cols, upper_cols = slab_items
        bottom_blocks, top_blocks = split_slab(slab_nodes, next_plane, degree)
        local_bottom = jnp.einsum("ij,ejb->eib", stiff_f32, bottom_blocks.astype(jnp.float32), precision=highest) * slab_scale[:4, None, None]
        local_top = jnp.einsum("ij,ejb->eib", stiff_f32, top_blocks.astype(jnp.float32), precision=highest) * slab_scale[4:, None, None]
        results = jnp.concatenate([local_bottom + scatter_ref(upper_proj, below_coef, upper_cols), local_top + scatter_ref(lower_proj, own_coef, lower_cols)])
        summed = assemble_blocks(results, degree)
        return summed[:-1], summed[-1]

    inner_nodes, rim_planes = lax.map(one_slab, (nodal_field, next_planes, scales, lower_slabs, upper_slabs, scaled, below_scaled, own_columns, upper_columns))
    assembled = inner_nodes.at[:, 0].add(jnp.roll(rim_planes, 1, axis=0))
    return mass_nodes * (assembled + local_potential * nodal_field.astype(jnp.float32))


def reference(wave_in, mass_scale, potential, elem_scale, stiffness, proj_lower, proj_upper, kb_coef, atom_column, chan_count, upper_column):
    degree = ORDER
    extent = 2 * degree
    band_count = wave_in.shape[-1]
    nodal_field = wave_in.reshape(N_SPACE, extent, extent, extent, band_count)
    mass_nodes = mass_scale.reshape(N_SPACE, extent, extent, extent, 1)
    local_potential = potential.reshape(N_SPACE, extent, extent, extent, 1)
    scales = elem_scale.reshape(N_SPACE, 8)
    lower_slabs = proj_lower.reshape(N_SPACE, ATOM_DEV, ELN, CH)
    upper_slabs = proj_upper.reshape(N_SPACE, ATOM_DEV, ELN, CH)
    live_channels = (jnp.arange(CH, dtype=jnp.int32)[None, :] < chan_count[:, None]).astype(jnp.float32)
    weights = (kb_coef * live_channels).reshape(N_SPACE, ATOM_DEV, CH)
    own_columns = atom_column.reshape(N_SPACE, ATOM_DEV)
    upper_columns = upper_column.reshape(N_SPACE, ATOM_DEV)
    initial = nodal_field.astype(jnp.float32)
    scaled_start = (mass_nodes * initial).astype(jnp.bfloat16)
    image_one = operator_ref(scaled_start, stiffness, scales, mass_nodes, local_potential, lower_slabs, upper_slabs, weights, own_columns, upper_columns, degree)
    step_one = ((image_one - spectrum_center * initial) / spectrum_half).astype(jnp.bfloat16)
    scaled_step = (mass_nodes * step_one.astype(jnp.float32)).astype(jnp.bfloat16)
    image_two = operator_ref(scaled_step, stiffness, scales, mass_nodes, local_potential, lower_slabs, upper_slabs, weights, own_columns, upper_columns, degree)
    filtered = (2.0 * (image_two - spectrum_center * step_one.astype(jnp.float32)) / spectrum_half - initial).astype(jnp.bfloat16)
    coefficients = coefficient_sums(filtered, lower_slabs, upper_slabs, own_columns, upper_columns, degree)
    return filtered.reshape(wave_in.shape), coefficients.reshape(N_SPACE * ATOM_DEV, CH, band_count)
```

```python
import functools

import jax
import jax.numpy as jnp
from jax import lax
from jax.experimental import pallas as pl
from jax.experimental.pallas import tpu as pltpu
from jax.sharding import PartitionSpec as P

MESH = pl.DeviceIdType.MESH
F32 = jnp.float32
BF16 = jnp.bfloat16

DEPTH = 768
MAIN = 576
FACE = 192
EDGE0 = 720
COEF0 = 736
NODES = 729
CH = 32


def node_selector():
    row = lax.broadcasted_iota(jnp.int32, (DEPTH, 128), 0)
    face = row - MAIN
    edge = row - EDGE0
    spot = jnp.bitwise_and(face, 15)
    old_main = (row >> 6) * 81 + jnp.bitwise_and(row >> 3, 7) * 9 + jnp.bitwise_and(row, 7)
    old_face = (face >> 4) * 81 + jnp.where(spot < 8, 72 + spot, (spot - 8) * 9 + 8)
    old_edge = jnp.where(edge < 9, edge * 81 + 80, -1)
    old = jnp.where(row < MAIN, old_main, jnp.where(row < EDGE0, old_face, old_edge))
    column = lax.broadcasted_iota(jnp.int32, (DEPTH, 128), 1)
    pieces = []
    for part in range(6):
        pieces.append((old == column + part * 128).astype(F32).astype(BF16))
    return jnp.concatenate(pieces, axis=1)[:, :NODES]


def dot(left, right):
    return jnp.dot(left, right, preferred_element_type=F32)


def kernel(
    wave_hbm, mass_hbm, pot_hbm, scale, stiff_hbm, lower_hbm, upper_hbm, kb, atom_col, count, upper_col,
    out_hbm, coef_out,
    wave, mass, pot, stiff, lower, upper, out_v,
    sel, kp, lp, lpt, up, upt, massb, potb, wv, wf, rim, zl, stepv,
    a_plane, a_held, b_rim, b_coef, send_plane, send_held, send_rim, send_coef,
    load_sem, store_sem, send_sem, recv_sem,
):
    me = lax.axis_index("space")
    n = lax.axis_size("space")
    right, left = lax.rem(me + 1, n), lax.rem(me + n - 1, n)

    loads = []
    for slot, (source, target) in enumerate(
        [(mass_hbm, mass), (wave_hbm, wave), (upper_hbm, upper), (stiff_hbm, stiff), (lower_hbm, lower), (pot_hbm, pot)]
    ):
        copy = pltpu.make_async_copy(source, target, load_sem.at[slot])
        copy.start()
        loads.append(copy)

    barrier = pltpu.get_barrier_semaphore()
    for neighbour in (left, right):
        pl.semaphore_signal(barrier, inc=1, device_id={"space": neighbour}, device_id_type=MESH)

    def remote(source, target, slot, neighbour):
        return pltpu.make_async_remote_copy(
            src_ref=source,
            dst_ref=target,
            send_sem=send_sem.at[slot],
            recv_sem=recv_sem.at[slot],
            device_id={"space": neighbour},
            device_id_type=MESH,
        )

    sel[...] = node_selector()
    for layer in range(2):
        for ab in range(4):
            rim[layer, ab, 160:192] = jnp.zeros((32, 128), BF16)

    def spread(source, target, planes):
        turned = jnp.transpose(source[...]).reshape(2, 8, 2, 8, 16)
        for p in planes:
            for a in range(2):
                for b in range(2):
                    block = turned[a, :, b, :, p : p + 1]
                    target[2 * a + b, p * 64 : p * 64 + 64] = jnp.broadcast_to(block, (8, 8, 128)).reshape(64, 128)

    def wave_block(p, a):
        both = wave[p, 8 * a : 8 * a + 8].astype(F32)
        return [both[:, 8 * b : 8 * b + 8].reshape(64, 128) for b in range(2)]

    def put_field(ab, p, value):
        rounded = value.astype(BF16)
        wv[ab, p * 64 : p * 64 + 64] = rounded
        wf[ab, p * 64 : p * 64 + 64] = rounded.astype(F32)

    def build_rim(layer):
        for a in range(2):
            for b in range(2):
                ab = 2 * a + b
                for i in range(9):
                    at = (8 * layer + i) * 64
                    j_face = wf[2 * (1 - a) + b, at : at + 8]
                    l_face = wf[2 * a + (1 - b), pl.ds(at, 8, stride=8)]
                    rim[layer, ab, i * 16 : i * 16 + 16] = jnp.concatenate([j_face, l_face], axis=0).astype(BF16)
                other = 2 * (1 - a) + (1 - b)
                edge = wf[other, pl.ds(8 * layer * 64, 8, stride=64)]
                last = wf[other, (8 * layer + 8) * 64 : (8 * layer + 8) * 64 + 8]
                rim[layer, ab, 144:160] = jnp.concatenate([edge, last], axis=0).astype(BF16)

    def bottom_operand(ab):
        return jnp.concatenate([wv[ab, 0:MAIN], rim[0, ab]], axis=0)

    def top_operand(ab, plane_slot):
        return jnp.concatenate([wv[ab, 512:1024], a_plane[plane_slot, ab], rim[1, ab]], axis=0)

    channel = lax.broadcasted_iota(jnp.int32, (CH, CH), 1)
    square = lax.broadcasted_iota(jnp.int32, (CH, CH), 0) == channel
    live = jnp.logical_and(square, channel < count[0])
    weight = jnp.sum(jnp.where(live, jnp.broadcast_to(kb[...], (CH, CH)), 0.0), axis=1, keepdims=True)

    loads[0].wait()
    spread(mass, massb, range(16))
    loads[1].wait()

    def start_field(planes):
        for p in planes:
            for a in range(2):
                for b, block in enumerate(wave_block(p, a)):
                    put_field(2 * a + b, p, massb[2 * a + b, p * 64 : p * 64 + 64] * block)

    start_field(range(0, 1))

    def send_plane_of(turn):
        for ab in range(4):
            send_plane[turn, ab] = wv[ab, 0:64]
        copy = remote(send_plane.at[turn], a_plane.at[turn], 4 * turn, left)
        copy.start()
        return copy

    def send_held_of(turn):
        send_held[turn] = dot(upt[...], bottom_operand(upper_col[0]))
        copy = remote(send_held.at[turn], a_held.at[turn], 4 * turn + 1, left)
        copy.start()
        return copy

    pl.semaphore_wait(barrier, 2)
    copies = [send_plane_of(0)]
    start_field(range(1, 9))
    build_rim(0)

    def turn_over(source, straight, across):
        picked = dot(sel[...], source[0])
        straight[...] = picked.astype(BF16)
        wide = jnp.concatenate([picked, jnp.zeros((DEPTH, 128 - CH), F32)], axis=1)
        across[...] = jnp.transpose(wide)[:CH].astype(BF16)

    loads[2].wait()
    turn_over(upper, up, upt)
    copies.append(send_held_of(0))
    start_field(range(9, 16))
    loads[3].wait()
    half = dot(sel[...], stiff[...]).astype(BF16)
    kp[...] = lax.dot_general(half, sel[...], (((1,), (1,)), ((), ())), preferred_element_type=F32).astype(BF16)
    loads[4].wait()
    turn_over(lower, lp, lpt)
    kp[:, COEF0:] = lp[...]
    loads[5].wait()
    spread(pot, potb, range(16))

    def layer_product(layer, rows, operands):
        for pair in range(2):
            both = jnp.concatenate(operands[2 * pair : 2 * pair + 2], axis=1)
            for low, high in rows:
                product = dot(kp[low:high], both)
                for k in range(2):
                    ab = 2 * pair + k
                    zl[layer, ab, low:high] = product[:, 128 * k : 128 * k + 128] * scale[layer, ab // 2, ab % 2]

    def bottom_product():
        layer_product(0, [(0, COEF0)], [bottom_operand(ab) for ab in range(4)])

    def add_rims(layer, planes):
        for i in planes:
            for a in range(2):
                for b in range(2):
                    ab = 2 * a + b
                    j_face = zl[layer, ab, MAIN + i * 16 : MAIN + i * 16 + 8]
                    l_face = zl[layer, ab, MAIN + i * 16 + 8 : MAIN + i * 16 + 16]
                    edge = zl[layer, ab, EDGE0 + i : EDGE0 + i + 1]
                    j_at = 2 * (1 - a) + b
                    l_at = 2 * a + (1 - b)
                    e_at = 2 * (1 - a) + (1 - b)
                    zl[layer, j_at, i * 64 : i * 64 + 8] = zl[layer, j_at, i * 64 : i * 64 + 8] + j_face
                    rows = pl.ds(i * 64, 8, stride=8)
                    zl[layer, l_at, rows] = zl[layer, l_at, rows] + l_face
                    zl[layer, e_at, i * 64 : i * 64 + 1] = zl[layer, e_at, i * 64 : i * 64 + 1] + edge

    def top_coef(turn, arrive):
        for ab in range(4):
            wf[ab, 1024:1088] = a_plane[turn, ab].astype(F32)
        build_rim(1)
        at = atom_col[0]
        own = dot(lpt[...], top_operand(at, turn))
        arrive.wait_recv()
        return own + a_held[turn]

    def elementwise(turn, planes):
        for p in planes:
            for a in range(2):
                waves = wave_block(p, a)
                filtered = []
                for b in range(2):
                    ab = 2 * a + b
                    rows = slice(p * 64, p * 64 + 64)
                    if p < 8:
                        total = zl[0, ab, p * 64 : p * 64 + 64]
                        if p == 0:
                            total = total + b_rim[turn, ab].astype(F32)
                    else:
                        total = zl[1, ab, (p - 8) * 64 : (p - 8) * 64 + 64]
                        if p == 8:
                            total = total + zl[0, ab, 512:576]
                    image = massb[ab, rows] * (total + potb[ab, rows] * wf[ab, rows])
                    if turn == 0:
                        step = ((image - waves[b]) * (1.0 / 6.0)).astype(BF16)
                        stepv[ab, rows] = step
                        put_field(ab, p, massb[ab, rows] * step.astype(F32))
                    else:
                        step = stepv[ab, rows].astype(F32)
                        value = (2.0 / 6.0) * (image - step) - waves[b]
                        put_field(ab, p, value)
                        filtered.append(value.reshape(8, 8, 128))
                if turn == 1:
                    out_v[p, 8 * a : 8 * a + 8] = jnp.concatenate(filtered, axis=1).astype(BF16)

    for turn in range(2):
        bottom_product()
        copies[-2].wait_recv()
        total = top_coef(turn, copies[-1]) * weight
        send_coef[turn] = total.astype(BF16)
        coef_copy = remote(send_coef.at[turn], b_coef.at[turn], 4 * turn + 2, right)
        coef_copy.start()
        for ab in range(4):
            inverse = jnp.full((CH, 128), 1.0, F32) / scale[1, ab // 2, ab % 2]
            inverse = jnp.where(atom_col[0] == ab, inverse, 0.0)
            rim[1, ab, 160:192] = (total * inverse).astype(BF16)
        operands = [top_operand(ab, turn) for ab in range(4)]
        layer_product(1, [(512, 576), (704, COEF0)], operands)
        add_rims(1, range(8, 9))
        for ab in range(4):
            send_rim[turn, ab] = zl[1, ab, 512:576].astype(BF16)
        rim_copy = remote(send_rim.at[turn], b_rim.at[turn], 4 * turn + 3, right)
        rim_copy.start()
        layer_product(1, [(0, 512), (MAIN, 704)], operands)
        add_rims(1, range(0, 8))
        elementwise(turn, range(9, 16))
        if turn == 1:
            early = pltpu.make_async_copy(out_v.at[9:16], out_hbm.at[9:16], store_sem.at[0])
            early.start()
        coef_copy.wait_recv()
        spread_coef = dot(up[:COEF0], b_coef[turn])
        for ab in range(4):
            chosen = jnp.where(upper_col[0] == ab, 1.0, 0.0)
            zl[0, ab, 0:COEF0] = zl[0, ab, 0:COEF0] + spread_coef * chosen
        add_rims(0, range(9))
        rim_copy.wait_recv()
        elementwise(turn, range(0, 9))
        build_rim(0)
        copies.append(coef_copy)
        copies.append(rim_copy)
        copies.append(send_plane_of(turn + 1))
        copies.append(send_held_of(turn + 1))

    late = pltpu.make_async_copy(out_v.at[0:9], out_hbm.at[0:9], store_sem.at[1])
    late.start()
    copies[-2].wait_recv()
    coef_out[0] = top_coef(2, copies[-1])
    for copy in copies:
        copy.wait_send()
    early.wait()
    late.wait()


def per_device(*arrays):
    wave_in = arrays[0]
    any_space = pl.BlockSpec(memory_space=pl.ANY)
    vmem = pl.BlockSpec(memory_space=pltpu.VMEM)
    smem = pl.BlockSpec(memory_space=pltpu.SMEM)
    return pl.pallas_call(
        kernel,
        out_shape=(
            jax.ShapeDtypeStruct(wave_in.shape, BF16),
            jax.ShapeDtypeStruct((1, CH, 128), F32),
        ),
        in_specs=[any_space, any_space, any_space, smem, any_space, any_space, any_space, vmem, smem, smem, smem],
        out_specs=(any_space, vmem),
        scratch_shapes=[
            pltpu.VMEM((16, 16, 16, 128), BF16),
            pltpu.VMEM((16, 256), F32),
            pltpu.VMEM((16, 256), F32),
            pltpu.VMEM((NODES, NODES), BF16),
            pltpu.VMEM((1, NODES, CH), BF16),
            pltpu.VMEM((1, NODES, CH), BF16),
            pltpu.VMEM((16, 16, 16, 128), BF16),
            pltpu.VMEM((DEPTH, NODES), BF16),
            pltpu.VMEM((DEPTH, DEPTH), BF16),
            pltpu.VMEM((DEPTH, CH), BF16),
            pltpu.VMEM((CH, DEPTH), BF16),
            pltpu.VMEM((DEPTH, CH), BF16),
            pltpu.VMEM((CH, DEPTH), BF16),
            pltpu.VMEM((4, 1024, 128), F32),
            pltpu.VMEM((4, 1024, 128), F32),
            pltpu.VMEM((4, 1024, 128), BF16),
            pltpu.VMEM((4, 1088, 128), F32),
            pltpu.VMEM((2, 4, FACE, 128), BF16),
            pltpu.VMEM((2, 4, COEF0, 128), F32),
            pltpu.VMEM((4, 1024, 128), BF16),
            pltpu.VMEM((3, 4, 64, 128), BF16),
            pltpu.VMEM((3, CH, 128), F32),
            pltpu.VMEM((2, 4, 64, 128), BF16),
            pltpu.VMEM((2, CH, 128), BF16),
            pltpu.VMEM((3, 4, 64, 128), BF16),
            pltpu.VMEM((3, CH, 128), F32),
            pltpu.VMEM((2, 4, 64, 128), BF16),
            pltpu.VMEM((2, CH, 128), BF16),
            pltpu.SemaphoreType.DMA((6,)),
            pltpu.SemaphoreType.DMA((2,)),
            pltpu.SemaphoreType.DMA((10,)),
            pltpu.SemaphoreType.DMA((10,)),
        ],
        compiler_params=pltpu.CompilerParams(
            collective_id=0, has_side_effects=True, vmem_limit_bytes=48 * 1024 * 1024
        ),
    )(*arrays)


def solution(mesh):
    in_specs = (
        P("space", None, None, "band"),
        P("space", None),
        P("space", None),
        P("space", None, None),
        P(),
        P("space", None, None),
        P("space", None, None),
        P("space", None),
        P("space"),
        P("space"),
        P("space"),
    )
    out_specs = (P("space", None, None, "band"), P("space", None, "band"))
    return jax.shard_map(
        per_device, mesh=mesh, in_specs=in_specs, out_specs=out_specs, check_vma=False
    )
```

```python
import functools

import jax
import jax.numpy as jnp
from jax import lax
from jax.experimental import pallas as pl
from jax.experimental.pallas import tpu as pltpu
from jax.sharding import PartitionSpec as P

MESH = pl.DeviceIdType.MESH
F32 = jnp.float32
BF16 = jnp.bfloat16

DEPTH = 768
MAIN = 576
FACE = 192
EDGE0 = 720
COEF0 = 736
NODES = 729
CH = 32


def node_selector():
    row = lax.broadcasted_iota(jnp.int32, (DEPTH, 128), 0)
    face = row - MAIN
    edge = row - EDGE0
    spot = jnp.bitwise_and(face, 15)
    old_main = (row >> 6) * 81 + jnp.bitwise_and(row >> 3, 7) * 9 + jnp.bitwise_and(row, 7)
    old_face = (face >> 4) * 81 + jnp.where(spot < 8, 72 + spot, (spot - 8) * 9 + 8)
    old_edge = jnp.where(edge < 9, edge * 81 + 80, -1)
    old = jnp.where(row < MAIN, old_main, jnp.where(row < EDGE0, old_face, old_edge))
    column = lax.broadcasted_iota(jnp.int32, (DEPTH, 128), 1)
    pieces = []
    for part in range(6):
        pieces.append((old == column + part * 128).astype(F32).astype(BF16))
    return jnp.concatenate(pieces, axis=1)[:, :NODES]


def dot(left, right):
    return jnp.dot(left, right, preferred_element_type=F32)


def dot_turned(left, right):
    return lax.dot_general(left, right, (((1,), (1,)), ((), ())), preferred_element_type=F32)


def kernel(
    wave_hbm, mass_hbm, pot_hbm, scale_hbm, stiff_hbm, lower_hbm, upper_hbm, kb_hbm, atom_col, count, upper_col,
    out_hbm, coef_hbm,
    wave, mass, pot, stiff, lower, upper, scale, kb, out_v, coef_v,
    sel, kp, both, both_t, massb, potb, mrim, wv, wf, rim, zl, stepv, pf, plane16, mass16, ez, e0,
    a_plane, a_held, a_edge, a_mass, a_gram, b_rim, b_coef,
    send_plane, send_held, send_edge, send_gram, send_rim, send_coef,
    load_sem, store_sem, send_sem, recv_sem,
):
    me = lax.axis_index("space")
    n = lax.axis_size("space")
    right, left = lax.rem(me + 1, n), lax.rem(me + n - 1, n)
    share = (1.0 / 6.0, 2.0 / 6.0)

    barrier = pltpu.get_barrier_semaphore()
    for neighbour in (left, right):
        pl.semaphore_signal(barrier, inc=1, device_id={"space": neighbour}, device_id_type=MESH)

    loads = []
    for slot, (source, target) in enumerate(
        [
            (mass_hbm, mass),
            (wave_hbm, wave),
            (upper_hbm, upper),
            (lower_hbm, lower),
            (stiff_hbm, stiff),
            (pot_hbm, pot),
            (scale_hbm, scale),
            (kb_hbm, kb),
        ]
    ):
        copy = pltpu.make_async_copy(source, target, load_sem.at[slot])
        copy.start()
        loads.append(copy)

    copies = []

    def remote(source, target, slot, neighbour):
        copy = pltpu.make_async_remote_copy(
            src_ref=source,
            dst_ref=target,
            send_sem=send_sem.at[slot],
            recv_sem=recv_sem.at[slot],
            device_id={"space": neighbour},
            device_id_type=MESH,
        )
        copy.start()
        copies.append(copy)
        return copy

    sel[...] = node_selector()
    for layer in range(2):
        for ab in range(4):
            rim[layer, ab, 160:192] = jnp.zeros((32, 128), BF16)

    def spread(turned, target, planes):
        turned = turned.reshape(2, 8, 2, 8, turned.shape[-1])
        for p in planes:
            for a in range(2):
                for b in range(2):
                    block = turned[a, :, b, :, p : p + 1]
                    target[2 * a + b, p * 64 : p * 64 + 64] = jnp.broadcast_to(block, (8, 8, 128)).reshape(64, 128)

    def wave_block(p, a):
        both_b = wave[p, 8 * a : 8 * a + 8].astype(F32)
        return [both_b[:, 8 * b : 8 * b + 8].reshape(64, 128) for b in range(2)]

    def put_field(ab, p, value):
        rounded = value.astype(BF16)
        wv[ab, p * 64 : p * 64 + 64] = rounded
        wf[ab, p * 64 : p * 64 + 64] = rounded.astype(F32)

    def gather_rim(source, base, put):
        for a in range(2):
            for b in range(2):
                ab = 2 * a + b
                for i in range(9):
                    at = base + i * 64
                    j_face = source[2 * (1 - a) + b, at : at + 8]
                    l_face = source[2 * a + (1 - b), pl.ds(at, 8, stride=8)]
                    put(ab, i * 16, jnp.concatenate([j_face, l_face], axis=0))
                other = 2 * (1 - a) + (1 - b)
                edge = source[other, pl.ds(base, 8, stride=64)]
                last = source[other, base + 512 : base + 520]
                put(ab, 144, jnp.concatenate([edge, last], axis=0))

    def build_rim(layer):
        def put(ab, row, value):
            rim[layer, ab, row : row + 16] = value.astype(BF16)

        gather_rim(wf, 512 * layer, put)

    def bottom_operand(ab):
        return jnp.concatenate([wv[ab, 0:MAIN], rim[0, ab]], axis=0)

    def top_operand(ab):
        return jnp.concatenate([wv[ab, 512:1024], plane16[ab], rim[1, ab]], axis=0)

    loads[0].wait()
    spread(jnp.transpose(mass[...]), massb, range(16))
    loads[1].wait()

    def start_field(planes):
        for p in planes:
            for a in range(2):
                for b, block in enumerate(wave_block(p, a)):
                    put_field(2 * a + b, p, massb[2 * a + b, p * 64 : p * 64 + 64] * block)

    def send_held_of(turn):
        send_held[turn] = dot(both_t[0:CH], bottom_operand(upper_col[0]))
        return remote(send_held.at[turn], a_held.at[turn], 3 + turn, left)

    start_field(range(0, 1))
    for ab in range(4):
        send_plane[0, ab] = wv[ab, 0:64]
    pl.semaphore_wait(barrier, 2)
    plane_copy = remote(send_plane.at[0], a_plane.at[0], 0, left)
    loads[2].wait()
    loads[3].wait()
    turned = dot_turned(jnp.concatenate([upper[0], lower[0]], axis=0), sel[...])
    both_t[...] = turned.astype(BF16)
    start_field(range(1, 9))
    build_rim(0)
    held_copy = send_held_of(0)
    both[...] = jnp.transpose(jnp.concatenate([turned, jnp.zeros((64, DEPTH), F32)], axis=0)).astype(BF16)
    loads[4].wait()
    half = dot(sel[...], stiff[...]).astype(BF16)
    kp[...] = dot_turned(half, sel[...]).astype(BF16)
    kp[:, COEF0:] = both[:, CH : 2 * CH]
    start_field(range(9, 16))
    for slot in (5, 6, 7):
        loads[slot].wait()
    spread(jnp.transpose(pot[...]), potb, range(16))

    channel = lax.broadcasted_iota(jnp.int32, (CH, CH), 1)
    square = lax.broadcasted_iota(jnp.int32, (CH, CH), 0) == channel
    live = jnp.logical_and(square, channel < count[0])
    weight = jnp.sum(jnp.where(live, jnp.broadcast_to(kb[...], (CH, CH)), 0.0), axis=1, keepdims=True)

    def scale_of(layer, ab, rows):
        return jnp.broadcast_to(scale[layer, ab // 2 : ab // 2 + 1, ab % 2 : ab % 2 + 1], (rows, 128))

    def chosen(column, ab):
        return jnp.where(column[0] == ab, 1.0, 0.0)

    def layer_product(layer, rows, operands):
        for pair in range(2):
            wide = jnp.concatenate(operands[2 * pair : 2 * pair + 2], axis=1)
            for low, high in rows:
                product = dot(kp[low:high], wide)
                for k in range(2):
                    ab = 2 * pair + k
                    zl[layer, ab, low:high] = product[:, 128 * k : 128 * k + 128] * scale_of(layer, ab, high - low)

    def add_rims(target, planes, face, edge_row):
        for i in planes:
            for a in range(2):
                for b in range(2):
                    ab = 2 * a + b
                    j_at, l_at, e_at = 2 * (1 - a) + b, 2 * a + (1 - b), 2 * (1 - a) + (1 - b)
                    j_face = target[ab, face + i * 16 : face + i * 16 + 8]
                    l_face = target[ab, face + i * 16 + 8 : face + i * 16 + 16]
                    edge = target[ab, edge_row + i : edge_row + i + 1]
                    target[j_at, i * 64 : i * 64 + 8] = target[j_at, i * 64 : i * 64 + 8] + j_face
                    rows = pl.ds(i * 64, 8, stride=8)
                    target[l_at, rows] = target[l_at, rows] + l_face
                    target[e_at, i * 64 : i * 64 + 1] = target[e_at, i * 64 : i * 64 + 1] + edge

    def layer_rims(layer, planes):
        add_rims(zl.at[layer], planes, MAIN, EDGE0)

    def set_up():
        for ab in range(4):
            part = chosen(upper_col, ab)
            ez[ab, 0:64] = both[0:64].astype(F32) * part
            ez[ab, 64:80] = both[MAIN : MAIN + 16].astype(F32) * part
            ez[ab, 80:96] = both[EDGE0 : EDGE0 + 16].astype(F32) * part
        add_rims(ez, range(1), 64, 80)
        placed = jnp.transpose(jnp.concatenate([ez[ab, 0:64] for ab in range(4)], axis=0))
        send_edge[...] = placed[0:CH].astype(BF16)
        sent = [remote(send_edge, a_edge, 6, left), remote(mass.at[0:8], a_mass, 7, left)]

        def put(ab, row, value):
            mrim[ab, row : row + 16] = value

        for ab in range(4):
            mrim[ab, 160:192] = jnp.zeros((32, 128), F32)
        gather_rim(massb, 0, put)
        at = upper_col[0]
        node_mass = jnp.concatenate([massb[at, 0:MAIN], mrim[at]], axis=0)
        wide = both[...].astype(F32) * node_mass
        send_gram[0] = dot(both_t[0:CH], (wide * node_mass).astype(BF16)) * share[0]
        send_gram[1] = dot(both_t[0:CH], wide.astype(BF16)) * share[1]
        sent.append(remote(send_gram, a_gram, 8, left))
        return sent

    def take_set_up(sent):
        sent[0].wait_recv()
        sent[1].wait_recv()
        wide = jnp.concatenate([a_edge[...].astype(F32), jnp.zeros((128 - CH, 256), F32)], axis=0)
        e0[...] = jnp.transpose(wide)[:, 0:CH].astype(BF16)
        spread(jnp.transpose(a_mass[...]), mass16, range(1))

    def finish_plane(turn):
        before = turn - 1
        coef = send_coef[before]
        placed = dot(e0[...], coef)
        shares = []
        parts = []
        for ab in range(4):
            edge_sum = send_rim[before, ab].astype(F32)
            amount = mass16[ab] * share[before]
            parts.append(amount * (edge_sum + placed[64 * ab : 64 * ab + 64]))
            shares.append((amount * edge_sum * mass16[ab] if turn == 1 else amount * edge_sum).astype(BF16))
        held = dot(a_edge[...], jnp.concatenate(shares, axis=0))
        held = held + jnp.dot(
            a_gram[before, :, 0:CH], coef.astype(F32), preferred_element_type=F32, precision=lax.Precision.HIGHEST
        )
        return parts, held

    def top_coef(turn, plane_copy, held_copy, setting):
        if turn > 0:
            if turn == 1:
                take_set_up(setting)
                setting[2].wait_recv()
            parts, extra = finish_plane(turn)
        plane_copy.wait_recv()
        for ab in range(4):
            value = a_plane[turn, ab].astype(F32)
            if turn > 0:
                value = value + parts[ab]
            if turn == 1:
                value = mass16[ab] * value.astype(BF16).astype(F32)
            value = value.astype(BF16)
            plane16[ab] = value
            wf[ab, 1024:1088] = value.astype(F32)
        build_rim(1)
        own = dot(both_t[CH : 2 * CH], top_operand(atom_col[0]))
        held_copy.wait_recv()
        own = own + a_held[turn]
        return own if turn == 0 else own + extra

    def combine(turn, p, ab, total, wave_part):
        rows = slice(p * 64, p * 64 + 64)
        image = massb[ab, rows] * (total + potb[ab, rows] * wf[ab, rows])
        if turn == 0:
            return (image - wave_part) * share[0]
        return share[1] * (image - stepv[ab, rows].astype(F32)) - wave_part

    def keep(turn, p, a, values):
        if turn == 0:
            for b in range(2):
                ab = 2 * a + b
                step = values[b].astype(BF16)
                stepv[ab, p * 64 : p * 64 + 64] = step
                put_field(ab, p, massb[ab, p * 64 : p * 64 + 64] * step.astype(F32))
            return
        if p >= 8:
            for b in range(2):
                put_field(2 * a + b, p, values[b])
        pieces = [value.reshape(8, 8, 128) for value in values]
        out_v[p, 8 * a : 8 * a + 8] = jnp.concatenate(pieces, axis=1).astype(BF16)

    def top_planes(turn):
        for p in range(9, 16):
            for a in range(2):
                waves = wave_block(p, a)
                values = []
                for b in range(2):
                    ab = 2 * a + b
                    total = zl[1, ab, (p - 8) * 64 : (p - 8) * 64 + 64]
                    values.append(combine(turn, p, ab, total, waves[b]))
                keep(turn, p, a, values)

    def bottom_planes_partly(turn):
        for p in range(9):
            for a in range(2):
                waves = wave_block(p, a)
                for b in range(2):
                    ab = 2 * a + b
                    rows = slice(p * 64, p * 64 + 64)
                    total = zl[0, ab, rows]
                    if p == 8:
                        total = total + zl[1, ab, 0:64]
                    value = combine(turn, p, ab, total, waves[b])
                    pf[ab, rows] = value
                    if p == 0:
                        send_plane[turn + 1, ab] = value.astype(BF16)
                    put_field(ab, p, massb[ab, rows] * value if turn == 0 else value)

    def bottom_planes(turn):
        for p in range(9):
            for a in range(2):
                values = []
                for b in range(2):
                    ab = 2 * a + b
                    rows = slice(p * 64, p * 64 + 64)
                    extra = zl[0, ab, rows]
                    if p == 0:
                        extra = extra + b_rim[turn, ab].astype(F32)
                    values.append(pf[ab, rows] + massb[ab, rows] * share[turn] * extra)
                keep(turn, p, a, values)

    for turn in range(2):
        layer_product(0, [(0, COEF0)], [bottom_operand(ab) for ab in range(4)])
        layer_rims(0, range(9))
        if turn == 0:
            setting = set_up()
        total = top_coef(turn, plane_copy, held_copy, setting) * weight
        send_coef[turn] = total.astype(BF16)
        coef_copy = remote(send_coef.at[turn], b_coef.at[turn], 9 + turn, right)
        for ab in range(4):
            part = (total / scale_of(1, ab, CH)) * chosen(atom_col, ab)
            rim[1, ab, 160:192] = part.astype(BF16)
        operands = [top_operand(ab) for ab in range(4)]
        layer_product(1, [(512, 576), (704, COEF0)], operands)
        layer_rims(1, range(8, 9))
        for ab in range(4):
            send_rim[turn, ab] = zl[1, ab, 512:576].astype(BF16)
        rim_copy = remote(send_rim.at[turn], b_rim.at[turn], 11 + turn, right)
        layer_product(1, [(0, 512), (MAIN, 704)], operands)
        layer_rims(1, range(0, 8))
        bottom_planes_partly(turn)
        plane_copy = remote(send_plane.at[turn + 1], a_plane.at[turn + 1], turn + 1, left)
        build_rim(0)
        held_copy = send_held_of(turn + 1)
        top_planes(turn)
        if turn == 1:
            early = pltpu.make_async_copy(out_v.at[9:16], out_hbm.at[9:16], store_sem.at[0])
            early.start()
        coef_copy.wait_recv()
        spread_coef = dot(both[:COEF0, 0:CH], b_coef[turn])
        for ab in range(4):
            zl[0, ab, 0:COEF0] = spread_coef * chosen(upper_col, ab)
        layer_rims(0, range(9))
        rim_copy.wait_recv()
        bottom_planes(turn)
        if turn == 0:
            build_rim(0)

    late = pltpu.make_async_copy(out_v.at[0:9], out_hbm.at[0:9], store_sem.at[1])
    late.start()
    coef_v[0] = top_coef(2, plane_copy, held_copy, setting)
    last = pltpu.make_async_copy(coef_v, coef_hbm, store_sem.at[2])
    last.start()
    for copy in copies:
        copy.wait_send()
    early.wait()
    late.wait()
    last.wait()


def per_device(*arrays):
    arrays = list(arrays)
    wave_in = arrays[0]
    arrays[5] = jnp.swapaxes(arrays[5], 1, 2)
    arrays[6] = jnp.swapaxes(arrays[6], 1, 2)
    any_space = pl.BlockSpec(memory_space=pl.ANY)
    smem = pl.BlockSpec(memory_space=pltpu.SMEM)
    return pl.pallas_call(
        kernel,
        out_shape=(
            jax.ShapeDtypeStruct(wave_in.shape, BF16),
            jax.ShapeDtypeStruct((1, CH, 128), F32),
        ),
        in_specs=[any_space] * 8 + [smem] * 3,
        out_specs=(any_space, any_space),
        scratch_shapes=[
            pltpu.VMEM((16, 16, 16, 128), BF16),
            pltpu.VMEM((16, 256), F32),
            pltpu.VMEM((16, 256), F32),
            pltpu.VMEM((NODES, NODES), BF16),
            pltpu.VMEM((1, CH, NODES), BF16),
            pltpu.VMEM((1, CH, NODES), BF16),
            pltpu.VMEM((2, 2, 2), F32),
            pltpu.VMEM((1, CH), F32),
            pltpu.VMEM((16, 16, 16, 128), BF16),
            pltpu.VMEM((1, CH, 128), F32),
            pltpu.VMEM((DEPTH, NODES), BF16),
            pltpu.VMEM((DEPTH, DEPTH), BF16),
            pltpu.VMEM((DEPTH, 128), BF16),
            pltpu.VMEM((2 * CH, DEPTH), BF16),
            pltpu.VMEM((4, 1024, 128), F32),
            pltpu.VMEM((4, 1024, 128), F32),
            pltpu.VMEM((4, FACE, 128), F32),
            pltpu.VMEM((4, 1024, 128), BF16),
            pltpu.VMEM((4, 1088, 128), F32),
            pltpu.VMEM((2, 4, FACE, 128), BF16),
            pltpu.VMEM((2, 4, COEF0, 128), F32),
            pltpu.VMEM((4, 1024, 128), BF16),
            pltpu.VMEM((4, MAIN, 128), F32),
            pltpu.VMEM((4, 64, 128), BF16),
            pltpu.VMEM((4, 64, 128), F32),
            pltpu.VMEM((4, 96, 128), F32),
            pltpu.VMEM((256, CH), BF16),
            pltpu.VMEM((3, 4, 64, 128), BF16),
            pltpu.VMEM((3, CH, 128), F32),
            pltpu.VMEM((CH, 256), BF16),
            pltpu.VMEM((8, 256), F32),
            pltpu.VMEM((2, CH, 128), F32),
            pltpu.VMEM((2, 4, 64, 128), BF16),
            pltpu.VMEM((2, CH, 128), BF16),
            pltpu.VMEM((3, 4, 64, 128), BF16),
            pltpu.VMEM((3, CH, 128), F32),
            pltpu.VMEM((CH, 256), BF16),
            pltpu.VMEM((2, CH, 128), F32),
            pltpu.VMEM((2, 4, 64, 128), BF16),
            pltpu.VMEM((2, CH, 128), BF16),
            pltpu.SemaphoreType.DMA((8,)),
            pltpu.SemaphoreType.DMA((3,)),
            pltpu.SemaphoreType.DMA((13,)),
            pltpu.SemaphoreType.DMA((13,)),
        ],
        compiler_params=pltpu.CompilerParams(
            collective_id=0, has_side_effects=True, vmem_limit_bytes=63 * 1024 * 1024
        ),
    )(*arrays)


def solution(mesh):
    in_specs = (
        P("space", None, None, "band"),
        P("space", None),
        P("space", None),
        P("space", None, None),
        P(),
        P("space", None, None),
        P("space", None, None),
        P("space", None),
        P("space"),
        P("space"),
        P("space"),
    )
    out_specs = (P("space", None, None, "band"), P("space", None, "band"))
    return jax.shard_map(
        per_device, mesh=mesh, in_specs=in_specs, out_specs=out_specs, check_vma=False
    )
```

```python
import functools

import jax
import jax.numpy as jnp
from jax import lax
from jax.experimental import pallas as pl
from jax.experimental.pallas import tpu as pltpu
from jax.sharding import PartitionSpec as P

MESH = pl.DeviceIdType.MESH
F32 = jnp.float32
BF16 = jnp.bfloat16

DEPTH = 768
MAIN = 576
FACE = 192
EDGE0 = 720
COEF0 = 736
NODES = 729
CH = 32


def node_selector():
    row = lax.broadcasted_iota(jnp.int32, (DEPTH, 128), 0)
    face = row - MAIN
    edge = row - EDGE0
    spot = jnp.bitwise_and(face, 15)
    old_main = (row >> 6) * 81 + jnp.bitwise_and(row >> 3, 7) * 9 + jnp.bitwise_and(row, 7)
    old_face = (face >> 4) * 81 + jnp.where(spot < 8, 72 + spot, (spot - 8) * 9 + 8)
    old_edge = jnp.where(edge < 9, edge * 81 + 80, -1)
    old = jnp.where(row < MAIN, old_main, jnp.where(row < EDGE0, old_face, old_edge))
    column = lax.broadcasted_iota(jnp.int32, (DEPTH, 128), 1)
    pieces = []
    for part in range(6):
        pieces.append((old == column + part * 128).astype(F32).astype(BF16))
    return jnp.concatenate(pieces, axis=1)[:, :NODES]


def dot(left, right):
    return jnp.dot(left, right, preferred_element_type=F32)


def dot_turned(left, right):
    return lax.dot_general(left, right, (((1,), (1,)), ((), ())), preferred_element_type=F32)


def kernel(
    wave_hbm, mass_hbm, pot_hbm, scale_hbm, stiff_hbm, lower_hbm, upper_hbm, kb_hbm, atom_ref, count_ref, next_ref,
    out_hbm, coef_hbm,
    wave, mass, pot, stiff, lower, upper, scale, kb, out_v, coef_v,
    sel, kp, both, both_t, massb, potb, mrim, wv, wf, rim, zl, stepv, pf, plane16, mass16, ez, e0,
    a_plane, a_held, a_edge, a_mass, a_gram, b_rim, b_coef,
    send_plane, send_held, send_edge, send_gram, send_rim, send_coef,
    load_sem, store_sem, send_sem, recv_sem,
):
    me = lax.axis_index("space")
    n = lax.axis_size("space")
    right, left = lax.rem(me + 1, n), lax.rem(me + n - 1, n)
    share = (1.0 / 6.0, 2.0 / 6.0)
    atom_col, count, upper_col = atom_ref[0], count_ref[0], next_ref[0]

    barrier = pltpu.get_barrier_semaphore()
    for neighbour in (left, right):
        pl.semaphore_signal(barrier, inc=1, device_id={"space": neighbour}, device_id_type=MESH)

    loads = []
    for slot, (source, target) in enumerate(
        [
            (mass_hbm, mass),
            (upper_hbm, upper),
            (lower_hbm, lower),
            (wave_hbm.at[0:9], wave.at[0:9]),
            (stiff_hbm, stiff),
            (wave_hbm.at[9:16], wave.at[9:16]),
            (pot_hbm, pot),
            (scale_hbm, scale),
            (kb_hbm, kb),
        ]
    ):
        copy = pltpu.make_async_copy(source, target, load_sem.at[slot])
        copy.start()
        loads.append(copy)

    copies = []

    def remote(source, target, slot, neighbour):
        copy = pltpu.make_async_remote_copy(
            src_ref=source,
            dst_ref=target,
            send_sem=send_sem.at[slot],
            recv_sem=recv_sem.at[slot],
            device_id={"space": neighbour},
            device_id_type=MESH,
        )
        copy.start()
        copies.append(copy)
        return copy

    sel[...] = node_selector()
    for layer in range(2):
        for ab in range(4):
            rim[layer, ab, 160:192] = jnp.zeros((32, 128), BF16)

    def spread(turned, target, planes):
        turned = turned.reshape(2, 8, 2, 8, turned.shape[-1])
        for p in planes:
            for a in range(2):
                for b in range(2):
                    block = turned[a, :, b, :, p : p + 1]
                    target[2 * a + b, p * 64 : p * 64 + 64] = jnp.broadcast_to(block, (8, 8, 128)).reshape(64, 128)

    def wave_block(p, a):
        both_b = wave[p, 8 * a : 8 * a + 8].astype(F32)
        return [both_b[:, 8 * b : 8 * b + 8].reshape(64, 128) for b in range(2)]

    def put_field(ab, p, value):
        rounded = value.astype(BF16)
        wv[ab, p * 64 : p * 64 + 64] = rounded
        wf[ab, p * 64 : p * 64 + 64] = rounded.astype(F32)

    def gather_rim(source, base, put):
        for a in range(2):
            for b in range(2):
                ab = 2 * a + b
                for i in range(9):
                    at = base + i * 64
                    j_face = source[2 * (1 - a) + b, at : at + 8]
                    l_face = source[2 * a + (1 - b), pl.ds(at, 8, stride=8)]
                    put(ab, i * 16, jnp.concatenate([j_face, l_face], axis=0))
                other = 2 * (1 - a) + (1 - b)
                edge = source[other, pl.ds(base, 8, stride=64)]
                last = source[other, base + 512 : base + 520]
                put(ab, 144, jnp.concatenate([edge, last], axis=0))

    def build_rim(layer):
        def put(ab, row, value):
            rim[layer, ab, row : row + 16] = value.astype(BF16)

        gather_rim(wf, 512 * layer, put)

    def bottom_operand(ab):
        return jnp.concatenate([wv[ab, 0:MAIN], rim[0, ab]], axis=0)

    def top_operand(ab):
        return jnp.concatenate([wv[ab, 512:1024], plane16[ab], rim[1, ab]], axis=0)

    loads[0].wait()
    spread(jnp.transpose(mass[...]), massb, range(16))
    loads[1].wait()
    loads[2].wait()
    turned = dot_turned(jnp.concatenate([upper[0], lower[0]], axis=0), sel[...])
    both_t[...] = turned.astype(BF16)
    loads[3].wait()

    def start_field(planes):
        for p in planes:
            for a in range(2):
                for b, block in enumerate(wave_block(p, a)):
                    put_field(2 * a + b, p, massb[2 * a + b, p * 64 : p * 64 + 64] * block)

    def send_held_of(turn):
        send_held[turn] = dot(both_t[0:CH], bottom_operand(upper_col))
        return remote(send_held.at[turn], a_held.at[turn], 3 + turn, left)

    start_field(range(0, 1))
    for ab in range(4):
        send_plane[0, ab] = wv[ab, 0:64]
    start_field(range(1, 9))
    build_rim(0)
    send_held[0] = dot(both_t[0:CH], bottom_operand(upper_col))
    pl.semaphore_wait(barrier, 2)
    plane_copy = remote(send_plane.at[0], a_plane.at[0], 0, left)
    held_copy = remote(send_held.at[0], a_held.at[0], 3, left)
    both[...] = jnp.transpose(jnp.concatenate([turned, jnp.zeros((64, DEPTH), F32)], axis=0)).astype(BF16)
    loads[4].wait()
    spans = [(0, 256, slice(0, 384)), (256, 512, slice(256, NODES)), (512, DEPTH, slice(0, NODES))]
    half = jnp.concatenate([dot(sel[low:high, old], stiff[old]) for low, high, old in spans], axis=0).astype(BF16)
    for low, high, old in spans:
        kp[:, low:high] = dot_turned(half[:, old], sel[low:high, old]).astype(BF16)
    kp[:, COEF0:] = both[:, CH : 2 * CH]
    for slot in (5, 6, 7, 8):
        loads[slot].wait()
    start_field(range(9, 16))
    spread(jnp.transpose(pot[...]), potb, range(16))

    channel = lax.broadcasted_iota(jnp.int32, (CH, CH), 1)
    square = lax.broadcasted_iota(jnp.int32, (CH, CH), 0) == channel
    live = jnp.logical_and(square, channel < count)
    weight = jnp.sum(jnp.where(live, jnp.broadcast_to(kb[...], (CH, CH)), 0.0), axis=1, keepdims=True)

    def scale_of(layer, ab, rows):
        return jnp.broadcast_to(scale[layer, ab // 2 : ab // 2 + 1, ab % 2 : ab % 2 + 1], (rows, 128))

    def chosen(column, ab):
        return jnp.where(column == ab, 1.0, 0.0)

    def layer_product(layer, rows, operands):
        for pair in range(2):
            wide = jnp.concatenate(operands[2 * pair : 2 * pair + 2], axis=1)
            for low, high in rows:
                product = dot(kp[low:high], wide)
                for k in range(2):
                    ab = 2 * pair + k
                    zl[layer, ab, low:high] = product[:, 128 * k : 128 * k + 128] * scale_of(layer, ab, high - low)

    def add_rims(target, planes, face, edge_row):
        for i in planes:
            for a in range(2):
                for b in range(2):
                    ab = 2 * a + b
                    j_at, l_at, e_at = 2 * (1 - a) + b, 2 * a + (1 - b), 2 * (1 - a) + (1 - b)
                    j_face = target[ab, face + i * 16 : face + i * 16 + 8]
                    l_face = target[ab, face + i * 16 + 8 : face + i * 16 + 16]
                    edge = target[ab, edge_row + i : edge_row + i + 1]
                    target[j_at, i * 64 : i * 64 + 8] = target[j_at, i * 64 : i * 64 + 8] + j_face
                    rows = pl.ds(i * 64, 8, stride=8)
                    target[l_at, rows] = target[l_at, rows] + l_face
                    target[e_at, i * 64 : i * 64 + 1] = target[e_at, i * 64 : i * 64 + 1] + edge

    def layer_rims(layer, planes):
        add_rims(zl.at[layer], planes, MAIN, EDGE0)

    def set_up():
        for ab in range(4):
            part = chosen(upper_col, ab)
            ez[ab, 0:64] = both[0:64].astype(F32) * part
            ez[ab, 64:80] = both[MAIN : MAIN + 16].astype(F32) * part
            ez[ab, 80:96] = both[EDGE0 : EDGE0 + 16].astype(F32) * part
        add_rims(ez, range(1), 64, 80)
        placed = jnp.transpose(jnp.concatenate([ez[ab, 0:64] for ab in range(4)], axis=0))
        send_edge[...] = placed[0:CH].astype(BF16)
        sent = [remote(send_edge, a_edge, 6, left), remote(mass.at[0:8], a_mass, 7, left)]

        def put(ab, row, value):
            mrim[ab, row : row + 16] = value

        for ab in range(4):
            mrim[ab, 160:192] = jnp.zeros((32, 128), F32)
        gather_rim(massb, 0, put)
        at = upper_col
        node_mass = jnp.concatenate([massb[at, 0:MAIN], mrim[at]], axis=0)
        wide = both[...].astype(F32) * node_mass
        send_gram[0] = dot(both_t[0:CH], (wide * node_mass).astype(BF16)) * share[0]
        send_gram[1] = dot(both_t[0:CH], wide.astype(BF16)) * share[1]
        sent.append(remote(send_gram, a_gram, 8, left))
        return sent

    def take_set_up(sent):
        for copy in sent:
            copy.wait_recv()
        wide = jnp.concatenate([a_edge[...].astype(F32), jnp.zeros((128 - CH, 256), F32)], axis=0)
        e0[...] = jnp.transpose(wide)[:, 0:CH].astype(BF16)
        spread(jnp.transpose(a_mass[...]), mass16, range(1))

    def finish_plane(turn):
        before = turn - 1
        coef = send_coef[before]
        placed = dot(e0[...], coef)
        shares = []
        parts = []
        for ab in range(4):
            edge_sum = send_rim[before, ab].astype(F32)
            amount = mass16[ab] * share[before]
            parts.append(amount * (edge_sum + placed[64 * ab : 64 * ab + 64]))
            shares.append((amount * edge_sum * mass16[ab] if turn == 1 else amount * edge_sum).astype(BF16))
        held = dot(a_edge[...], jnp.concatenate(shares, axis=0))
        held = held + jnp.dot(
            a_gram[before, :, 0:CH], coef.astype(F32), preferred_element_type=F32, precision=lax.Precision.HIGHEST
        )
        return parts, held

    def top_coef(turn, plane_copy, held_copy, parts, extra):
        plane_copy.wait_recv()
        for ab in range(4):
            value = a_plane[turn, ab].astype(F32)
            if turn > 0:
                value = value + parts[ab]
            if turn == 1:
                value = mass16[ab] * value.astype(BF16).astype(F32)
            value = value.astype(BF16)
            plane16[ab] = value
            wf[ab, 1024:1088] = value.astype(F32)
        build_rim(1)
        own = dot(both_t[CH : 2 * CH], top_operand(atom_col))
        held_copy.wait_recv()
        own = own + a_held[turn]
        return own if turn == 0 else own + extra

    def combine(turn, p, ab, total, wave_part):
        rows = slice(p * 64, p * 64 + 64)
        image = massb[ab, rows] * (total + potb[ab, rows] * wf[ab, rows])
        if turn == 0:
            return (image - wave_part) * share[0]
        return share[1] * (image - stepv[ab, rows].astype(F32)) - wave_part

    def keep(turn, p, a, values):
        if turn == 0:
            for b in range(2):
                ab = 2 * a + b
                step = values[b].astype(BF16)
                stepv[ab, p * 64 : p * 64 + 64] = step
                put_field(ab, p, massb[ab, p * 64 : p * 64 + 64] * step.astype(F32))
            return
        if p >= 8:
            for b in range(2):
                put_field(2 * a + b, p, values[b])
        pieces = [value.reshape(8, 8, 128) for value in values]
        out_v[p, 8 * a : 8 * a + 8] = jnp.concatenate(pieces, axis=1).astype(BF16)

    def top_planes(turn):
        for p in range(9, 16):
            for a in range(2):
                waves = wave_block(p, a)
                values = []
                for b in range(2):
                    ab = 2 * a + b
                    total = zl[1, ab, (p - 8) * 64 : (p - 8) * 64 + 64]
                    values.append(combine(turn, p, ab, total, waves[b]))
                keep(turn, p, a, values)

    def bottom_planes_partly(turn):
        for p in range(9):
            for a in range(2):
                waves = wave_block(p, a)
                for b in range(2):
                    ab = 2 * a + b
                    rows = slice(p * 64, p * 64 + 64)
                    total = zl[0, ab, rows]
                    if p == 8:
                        total = total + zl[1, ab, 0:64]
                    value = combine(turn, p, ab, total, waves[b])
                    pf[ab, rows] = value
                    if p == 0:
                        send_plane[turn + 1, ab] = value.astype(BF16)
                    put_field(ab, p, massb[ab, rows] * value if turn == 0 else value)

    def bottom_planes(turn, planes):
        for p in planes:
            for a in range(2):
                values = []
                for b in range(2):
                    ab = 2 * a + b
                    rows = slice(p * 64, p * 64 + 64)
                    extra = zl[0, ab, rows]
                    if p == 0:
                        extra = extra + b_rim[turn, ab].astype(F32)
                    values.append(pf[ab, rows] + massb[ab, rows] * share[turn] * extra)
                keep(turn, p, a, values)

    def bottom_product():
        layer_product(0, [(0, COEF0)], [bottom_operand(ab) for ab in range(4)])
        layer_rims(0, range(9))

    parts, extra = None, None
    for turn in range(2):
        if turn == 0:
            bottom_product()
            setting = set_up()
        total = top_coef(turn, plane_copy, held_copy, parts, extra) * weight
        send_coef[turn] = total.astype(BF16)
        coef_copy = remote(send_coef.at[turn], b_coef.at[turn], 9 + turn, right)
        for ab in range(4):
            part = (total / scale_of(1, ab, CH)) * chosen(atom_col, ab)
            rim[1, ab, 160:192] = part.astype(BF16)
        operands = [top_operand(ab) for ab in range(4)]
        layer_product(1, [(512, 576), (704, COEF0)], operands)
        layer_rims(1, range(8, 9))
        for ab in range(4):
            send_rim[turn, ab] = zl[1, ab, 512:576].astype(BF16)
        rim_copy = remote(send_rim.at[turn], b_rim.at[turn], 11 + turn, right)
        if turn == 1:
            bottom_product()
        layer_product(1, [(0, 512), (MAIN, 704)], operands)
        layer_rims(1, range(0, 8))
        bottom_planes_partly(turn)
        plane_copy = remote(send_plane.at[turn + 1], a_plane.at[turn + 1], turn + 1, left)
        build_rim(0)
        held_copy = send_held_of(turn + 1)
        top_planes(turn)
        if turn == 1:
            early = pltpu.make_async_copy(out_v.at[9:16], out_hbm.at[9:16], store_sem.at[0])
            early.start()
        if turn == 0:
            take_set_up(setting)
        parts, extra = finish_plane(turn + 1)
        coef_copy.wait_recv()
        spread_coef = dot(both[:COEF0, 0:CH], b_coef[turn])
        for ab in range(4):
            zl[0, ab, 0:COEF0] = spread_coef * chosen(upper_col, ab)
        layer_rims(0, range(9))
        bottom_planes(turn, range(1, 9))
        if turn == 1:
            late = pltpu.make_async_copy(out_v.at[1:9], out_hbm.at[1:9], store_sem.at[1])
            late.start()
        rim_copy.wait_recv()
        bottom_planes(turn, range(0, 1))
        if turn == 0:
            build_rim(0)

    first = pltpu.make_async_copy(out_v.at[0:1], out_hbm.at[0:1], store_sem.at[3])
    first.start()
    coef_v[0] = top_coef(2, plane_copy, held_copy, parts, extra)
    last = pltpu.make_async_copy(coef_v, coef_hbm, store_sem.at[2])
    last.start()
    for copy in copies:
        copy.wait_send()
    early.wait()
    late.wait()
    first.wait()
    last.wait()


def hand_on(field, coef, field_out, coef_out, held, coef_held, sem):
    pairs = [(coef, coef_held, coef_out)]
    for part in range(4):
        planes = pl.ds(4 * part, 4)
        pairs.append((field.at[planes], held.at[planes], field_out.at[planes]))
    inward = [pltpu.make_async_copy(x, y, sem.at[k]) for k, (x, y, _) in enumerate(pairs)]
    outward = [pltpu.make_async_copy(y, z, sem.at[5 + k]) for k, (_, y, z) in enumerate(pairs)]
    for copy in inward:
        copy.start()
    for first, second in zip(inward, outward):
        first.wait()
        second.start()
    for copy in outward:
        copy.wait()


def per_device(*arrays):
    arrays = list(arrays)
    wave_in = arrays[0]
    arrays[5] = jnp.swapaxes(arrays[5], 1, 2)
    arrays[6] = jnp.swapaxes(arrays[6], 1, 2)
    any_space = pl.BlockSpec(memory_space=pl.ANY)
    results = pl.pallas_call(
        kernel,
        out_shape=(
            jax.ShapeDtypeStruct(wave_in.shape, BF16),
            jax.ShapeDtypeStruct((1, CH, 128), F32),
        ),
        in_specs=[any_space] * 8 + [pl.BlockSpec(memory_space=pltpu.SMEM)] * 3,
        out_specs=(any_space, any_space),
        scratch_shapes=[
            pltpu.VMEM((16, 16, 16, 128), BF16),
            pltpu.VMEM((16, 256), F32),
            pltpu.VMEM((16, 256), F32),
            pltpu.VMEM((NODES, NODES), BF16),
            pltpu.VMEM((1, CH, NODES), BF16),
            pltpu.VMEM((1, CH, NODES), BF16),
            pltpu.VMEM((2, 2, 2), F32),
            pltpu.VMEM((1, CH), F32),
            pltpu.VMEM((16, 16, 16, 128), BF16),
            pltpu.VMEM((1, CH, 128), F32),
            pltpu.VMEM((DEPTH, NODES), BF16),
            pltpu.VMEM((DEPTH, DEPTH), BF16),
            pltpu.VMEM((DEPTH, 128), BF16),
            pltpu.VMEM((2 * CH, DEPTH), BF16),
            pltpu.VMEM((4, 1024, 128), F32),
            pltpu.VMEM((4, 1024, 128), F32),
            pltpu.VMEM((4, FACE, 128), F32),
            pltpu.VMEM((4, 1024, 128), BF16),
            pltpu.VMEM((4, 1088, 128), F32),
            pltpu.VMEM((2, 4, FACE, 128), BF16),
            pltpu.VMEM((2, 4, COEF0, 128), F32),
            pltpu.VMEM((4, 1024, 128), BF16),
            pltpu.VMEM((4, MAIN, 128), F32),
            pltpu.VMEM((4, 64, 128), BF16),
            pltpu.VMEM((4, 64, 128), F32),
            pltpu.VMEM((4, 96, 128), F32),
            pltpu.VMEM((256, CH), BF16),
            pltpu.VMEM((3, 4, 64, 128), BF16),
            pltpu.VMEM((3, CH, 128), F32),
            pltpu.VMEM((CH, 256), BF16),
            pltpu.VMEM((8, 256), F32),
            pltpu.VMEM((2, CH, 128), F32),
            pltpu.VMEM((2, 4, 64, 128), BF16),
            pltpu.VMEM((2, CH, 128), BF16),
            pltpu.VMEM((3, 4, 64, 128), BF16),
            pltpu.VMEM((3, CH, 128), F32),
            pltpu.VMEM((CH, 256), BF16),
            pltpu.VMEM((2, CH, 128), F32),
            pltpu.VMEM((2, 4, 64, 128), BF16),
            pltpu.VMEM((2, CH, 128), BF16),
            pltpu.SemaphoreType.DMA((9,)),
            pltpu.SemaphoreType.DMA((4,)),
            pltpu.SemaphoreType.DMA((13,)),
            pltpu.SemaphoreType.DMA((13,)),
        ],
        compiler_params=pltpu.CompilerParams(
            collective_id=0, has_side_effects=True, vmem_limit_bytes=63 * 1024 * 1024
        ),
    )(*arrays)
    return pl.pallas_call(
        hand_on,
        out_shape=(
            jax.ShapeDtypeStruct(wave_in.shape, BF16),
            jax.ShapeDtypeStruct((1, CH, 128), F32),
        ),
        in_specs=[any_space] * 2,
        out_specs=(any_space, any_space),
        scratch_shapes=[
            pltpu.VMEM((16, 16, 16, 128), BF16),
            pltpu.VMEM((1, CH, 128), F32),
            pltpu.SemaphoreType.DMA((10,)),
        ],
    )(*results)


def solution(mesh):
    in_specs = (
        P("space", None, None, "band"),
        P("space", None),
        P("space", None),
        P("space", None, None),
        P(),
        P("space", None, None),
        P("space", None, None),
        P("space", None),
        P("space"),
        P("space"),
        P("space"),
    )
    out_specs = (P("space", None, None, "band"), P("space", None, "band"))
    return jax.shard_map(
        per_device, mesh=mesh, in_specs=in_specs, out_specs=out_specs, check_vma=False
    )
```

```python
import functools

import jax
import jax.numpy as jnp
from jax import lax
from jax.experimental import pallas as pl
from jax.experimental.pallas import tpu as pltpu
from jax.sharding import PartitionSpec as P

MESH = pl.DeviceIdType.MESH
F32 = jnp.float32
BF16 = jnp.bfloat16

DEPTH = 768
MAIN = 576
FACE = 192
EDGE0 = 720
COEF0 = 736
NODES = 729
CH = 32


def node_selector():
    row = lax.broadcasted_iota(jnp.int32, (DEPTH, 128), 0)
    face = row - MAIN
    edge = row - EDGE0
    spot = jnp.bitwise_and(face, 15)
    old_main = (row >> 6) * 81 + jnp.bitwise_and(row >> 3, 7) * 9 + jnp.bitwise_and(row, 7)
    old_face = (face >> 4) * 81 + jnp.where(spot < 8, 72 + spot, (spot - 8) * 9 + 8)
    old_edge = jnp.where(edge < 9, edge * 81 + 80, -1)
    old = jnp.where(row < MAIN, old_main, jnp.where(row < EDGE0, old_face, old_edge))
    column = lax.broadcasted_iota(jnp.int32, (DEPTH, 128), 1)
    pieces = []
    for part in range(6):
        pieces.append((old == column + part * 128).astype(F32).astype(BF16))
    return jnp.concatenate(pieces, axis=1)[:, :NODES]


def dot(left, right):
    return jnp.dot(left, right, preferred_element_type=F32)


def dot_turned(left, right):
    return lax.dot_general(left, right, (((1,), (1,)), ((), ())), preferred_element_type=F32)


def kernel(
    wave_hbm, mass_hbm, pot_hbm, scale_hbm, stiff_hbm, lower_hbm, upper_hbm, kb_hbm, atom_ref, count_ref, next_ref,
    out_hbm, coef_hbm,
    wave, mass, pot, stiff, lower, upper, scale, kb, out_v, coef_v,
    sel, kp, both, both_t, massb, potb, mrim, wv, wf, rim, zl, stepv, pf, plane16, mass16, ez, e0,
    a_plane, a_held, a_edge, a_mass, a_gram, b_rim, b_coef,
    send_plane, send_held, send_edge, send_gram, send_rim, send_coef,
    load_sem, store_sem, send_sem, recv_sem,
):
    me = lax.axis_index("space")
    n = lax.axis_size("space")
    right, left = lax.rem(me + 1, n), lax.rem(me + n - 1, n)
    share = (1.0 / 6.0, 2.0 / 6.0)
    atom_col, count, upper_col = atom_ref[0], count_ref[0], next_ref[0]

    barrier = pltpu.get_barrier_semaphore()
    for neighbour in (left, right):
        pl.semaphore_signal(barrier, inc=1, device_id={"space": neighbour}, device_id_type=MESH)

    loads = []
    for slot, (source, target) in enumerate(
        [
            (mass_hbm, mass),
            (upper_hbm, upper),
            (lower_hbm, lower),
            (wave_hbm.at[0:9], wave.at[0:9]),
            (stiff_hbm, stiff),
            (wave_hbm.at[9:16], wave.at[9:16]),
            (pot_hbm, pot),
            (scale_hbm, scale),
            (kb_hbm, kb),
        ]
    ):
        copy = pltpu.make_async_copy(source, target, load_sem.at[slot])
        copy.start()
        loads.append(copy)

    copies = []

    def remote(source, target, slot, neighbour):
        copy = pltpu.make_async_remote_copy(
            src_ref=source,
            dst_ref=target,
            send_sem=send_sem.at[slot],
            recv_sem=recv_sem.at[slot],
            device_id={"space": neighbour},
            device_id_type=MESH,
        )
        copy.start()
        copies.append(copy)
        return copy

    sel[...] = node_selector()
    for layer in range(2):
        for ab in range(4):
            rim[layer, ab, 160:192] = jnp.zeros((32, 128), BF16)

    def spread(turned, target, planes):
        turned = turned.reshape(2, 8, 2, 8, turned.shape[-1])
        for p in planes:
            for a in range(2):
                for b in range(2):
                    block = turned[a, :, b, :, p : p + 1]
                    target[2 * a + b, p * 64 : p * 64 + 64] = jnp.broadcast_to(block, (8, 8, 128)).reshape(64, 128)

    def wave_block(p, a):
        both_b = wave[p, 8 * a : 8 * a + 8].astype(F32)
        return [both_b[:, 8 * b : 8 * b + 8].reshape(64, 128) for b in range(2)]

    def put_field(ab, p, value):
        rounded = value.astype(BF16)
        wv[ab, p * 64 : p * 64 + 64] = rounded
        wf[ab, p * 64 : p * 64 + 64] = rounded.astype(F32)

    def gather_rim(source, base, put):
        for a in range(2):
            for b in range(2):
                ab = 2 * a + b
                for i in range(9):
                    at = base + i * 64
                    j_face = source[2 * (1 - a) + b, at : at + 8]
                    l_face = source[2 * a + (1 - b), pl.ds(at, 8, stride=8)]
                    put(ab, i * 16, jnp.concatenate([j_face, l_face], axis=0))
                other = 2 * (1 - a) + (1 - b)
                edge = source[other, pl.ds(base, 8, stride=64)]
                last = source[other, base + 512 : base + 520]
                put(ab, 144, jnp.concatenate([edge, last], axis=0))

    def build_rim(layer):
        def put(ab, row, value):
            rim[layer, ab, row : row + 16] = value.astype(BF16)

        gather_rim(wf, 512 * layer, put)

    def bottom_operand(ab):
        return jnp.concatenate([wv[ab, 0:MAIN], rim[0, ab]], axis=0)

    def top_operand(ab):
        return jnp.concatenate([wv[ab, 512:1024], plane16[ab], rim[1, ab]], axis=0)

    loads[0].wait()
    spread(jnp.transpose(mass[...]), massb, range(16))
    loads[1].wait()
    loads[2].wait()
    turned = dot_turned(jnp.concatenate([upper[0], lower[0]], axis=0), sel[...])
    both_t[...] = turned.astype(BF16)
    loads[3].wait()

    def start_field(planes):
        for p in planes:
            for a in range(2):
                for b, block in enumerate(wave_block(p, a)):
                    put_field(2 * a + b, p, massb[2 * a + b, p * 64 : p * 64 + 64] * block)

    def send_held_of(turn):
        send_held[turn] = dot(both_t[0:CH], bottom_operand(upper_col))
        return remote(send_held.at[turn], a_held.at[turn], 3 + turn, left)

    start_field(range(0, 1))
    for ab in range(4):
        send_plane[0, ab] = wv[ab, 0:64]
    start_field(range(1, 9))
    build_rim(0)
    send_held[0] = dot(both_t[0:CH], bottom_operand(upper_col))
    pl.semaphore_wait(barrier, 2)
    plane_copy = remote(send_plane.at[0], a_plane.at[0], 0, left)
    held_copy = remote(send_held.at[0], a_held.at[0], 3, left)
    both[...] = jnp.transpose(jnp.concatenate([turned, jnp.zeros((64, DEPTH), F32)], axis=0)).astype(BF16)
    loads[4].wait()
    spans = [(0, 256, slice(0, 384)), (256, 512, slice(256, NODES)), (512, DEPTH, slice(0, NODES))]
    half = jnp.concatenate([dot(sel[low:high, old], stiff[old]) for low, high, old in spans], axis=0).astype(BF16)
    for low, high, old in spans:
        kp[:, low:high] = dot_turned(half[:, old], sel[low:high, old]).astype(BF16)
    kp[:, COEF0:] = both[:, CH : 2 * CH]
    for slot in (5, 6, 7, 8):
        loads[slot].wait()
    start_field(range(9, 16))
    spread(jnp.transpose(pot[...]), potb, range(16))

    channel = lax.broadcasted_iota(jnp.int32, (CH, CH), 1)
    square = lax.broadcasted_iota(jnp.int32, (CH, CH), 0) == channel
    live = jnp.logical_and(square, channel < count)
    weight = jnp.sum(jnp.where(live, jnp.broadcast_to(kb[...], (CH, CH)), 0.0), axis=1, keepdims=True)

    def scale_of(layer, ab, rows):
        return jnp.broadcast_to(scale[layer, ab // 2 : ab // 2 + 1, ab % 2 : ab % 2 + 1], (rows, 128))

    def chosen(column, ab):
        return jnp.where(column == ab, 1.0, 0.0)

    def layer_product(layer, rows, operands):
        for pair in range(2):
            wide = jnp.concatenate(operands[2 * pair : 2 * pair + 2], axis=1)
            for low, high in rows:
                product = dot(kp[low:high], wide)
                for k in range(2):
                    ab = 2 * pair + k
                    zl[layer, ab, low:high] = product[:, 128 * k : 128 * k + 128] * scale_of(layer, ab, high - low)

    def add_rims(target, planes, face, edge_row):
        for i in planes:
            for a in range(2):
                for b in range(2):
                    ab = 2 * a + b
                    j_at, l_at, e_at = 2 * (1 - a) + b, 2 * a + (1 - b), 2 * (1 - a) + (1 - b)
                    j_face = target[ab, face + i * 16 : face + i * 16 + 8]
                    l_face = target[ab, face + i * 16 + 8 : face + i * 16 + 16]
                    edge = target[ab, edge_row + i : edge_row + i + 1]
                    target[j_at, i * 64 : i * 64 + 8] = target[j_at, i * 64 : i * 64 + 8] + j_face
                    rows = pl.ds(i * 64, 8, stride=8)
                    target[l_at, rows] = target[l_at, rows] + l_face
                    target[e_at, i * 64 : i * 64 + 1] = target[e_at, i * 64 : i * 64 + 1] + edge

    def layer_rims(layer, planes):
        add_rims(zl.at[layer], planes, MAIN, EDGE0)

    def set_up():
        for ab in range(4):
            part = chosen(upper_col, ab)
            ez[ab, 0:64] = both[0:64].astype(F32) * part
            ez[ab, 64:80] = both[MAIN : MAIN + 16].astype(F32) * part
            ez[ab, 80:96] = both[EDGE0 : EDGE0 + 16].astype(F32) * part
        add_rims(ez, range(1), 64, 80)
        placed = jnp.transpose(jnp.concatenate([ez[ab, 0:64] for ab in range(4)], axis=0))
        send_edge[...] = placed[0:CH].astype(BF16)
        sent = [remote(send_edge, a_edge, 6, left), remote(mass.at[0:8], a_mass, 7, left)]

        def put(ab, row, value):
            mrim[ab, row : row + 16] = value

        for ab in range(4):
            mrim[ab, 160:192] = jnp.zeros((32, 128), F32)
        gather_rim(massb, 0, put)
        at = upper_col
        node_mass = jnp.concatenate([massb[at, 0:MAIN], mrim[at]], axis=0)
        wide = both[...].astype(F32) * node_mass
        send_gram[0] = dot(both_t[0:CH], (wide * node_mass).astype(BF16)) * share[0]
        send_gram[1] = dot(both_t[0:CH], wide.astype(BF16)) * share[1]
        sent.append(remote(send_gram, a_gram, 8, left))
        return sent

    def take_set_up(sent):
        for copy in sent:
            copy.wait_recv()
        wide = jnp.concatenate([a_edge[...].astype(F32), jnp.zeros((128 - CH, 256), F32)], axis=0)
        e0[...] = jnp.transpose(wide)[:, 0:CH].astype(BF16)
        spread(jnp.transpose(a_mass[...]), mass16, range(1))

    def finish_plane(turn):
        before = turn - 1
        coef = send_coef[before]
        placed = dot(e0[...], coef)
        shares = []
        parts = []
        for ab in range(4):
            edge_sum = send_rim[before, ab].astype(F32)
            amount = mass16[ab] * share[before]
            parts.append(amount * (edge_sum + placed[64 * ab : 64 * ab + 64]))
            shares.append((amount * edge_sum * mass16[ab] if turn == 1 else amount * edge_sum).astype(BF16))
        held = dot(a_edge[...], jnp.concatenate(shares, axis=0))
        held = held + jnp.dot(
            a_gram[before, :, 0:CH], coef.astype(F32), preferred_element_type=F32, precision=lax.Precision.HIGHEST
        )
        return parts, held

    def top_coef(turn, plane_copy, held_copy, parts, extra):
        plane_copy.wait_recv()
        for ab in range(4):
            value = a_plane[turn, ab].astype(F32)
            if turn > 0:
                value = value + parts[ab]
            if turn == 1:
                value = mass16[ab] * value.astype(BF16).astype(F32)
            value = value.astype(BF16)
            plane16[ab] = value
            wf[ab, 1024:1088] = value.astype(F32)
        build_rim(1)
        own = dot(both_t[CH : 2 * CH], top_operand(atom_col))
        held_copy.wait_recv()
        own = own + a_held[turn]
        return own if turn == 0 else own + extra

    def combine(turn, p, ab, total, wave_part):
        rows = slice(p * 64, p * 64 + 64)
        image = massb[ab, rows] * (total + potb[ab, rows] * wf[ab, rows])
        if turn == 0:
            return (image - wave_part) * share[0]
        return share[1] * (image - stepv[ab, rows].astype(F32)) - wave_part

    def keep(turn, p, a, values):
        if turn == 0:
            for b in range(2):
                ab = 2 * a + b
                step = values[b].astype(BF16)
                stepv[ab, p * 64 : p * 64 + 64] = step
                put_field(ab, p, massb[ab, p * 64 : p * 64 + 64] * step.astype(F32))
            return
        if p >= 8:
            for b in range(2):
                put_field(2 * a + b, p, values[b])
        pieces = [value.reshape(8, 8, 128) for value in values]
        out_v[p, 8 * a : 8 * a + 8] = jnp.concatenate(pieces, axis=1).astype(BF16)

    def top_planes(turn):
        for p in range(9, 16):
            for a in range(2):
                waves = wave_block(p, a)
                values = []
                for b in range(2):
                    ab = 2 * a + b
                    total = zl[1, ab, (p - 8) * 64 : (p - 8) * 64 + 64]
                    values.append(combine(turn, p, ab, total, waves[b]))
                keep(turn, p, a, values)

    def bottom_planes_partly(turn):
        for p in range(9):
            for a in range(2):
                waves = wave_block(p, a)
                for b in range(2):
                    ab = 2 * a + b
                    rows = slice(p * 64, p * 64 + 64)
                    total = zl[0, ab, rows]
                    if p == 8:
                        total = total + zl[1, ab, 0:64]
                    value = combine(turn, p, ab, total, waves[b])
                    pf[ab, rows] = value
                    if p == 0:
                        send_plane[turn + 1, ab] = value.astype(BF16)
                    put_field(ab, p, massb[ab, rows] * value if turn == 0 else value)

    def bottom_planes(turn, planes):
        for p in planes:
            for a in range(2):
                values = []
                for b in range(2):
                    ab = 2 * a + b
                    rows = slice(p * 64, p * 64 + 64)
                    extra = zl[0, ab, rows]
                    if p == 0:
                        extra = extra + b_rim[turn, ab].astype(F32)
                    values.append(pf[ab, rows] + massb[ab, rows] * share[turn] * extra)
                keep(turn, p, a, values)

    def bottom_product():
        layer_product(0, [(0, COEF0)], [bottom_operand(ab) for ab in range(4)])
        layer_rims(0, range(9))

    parts, extra = None, None
    for turn in range(2):
        if turn == 0:
            bottom_product()
            setting = set_up()
        total = top_coef(turn, plane_copy, held_copy, parts, extra) * weight
        send_coef[turn] = total.astype(BF16)
        coef_copy = remote(send_coef.at[turn], b_coef.at[turn], 9 + turn, right)
        for ab in range(4):
            part = (total / scale_of(1, ab, CH)) * chosen(atom_col, ab)
            rim[1, ab, 160:192] = part.astype(BF16)
        operands = [top_operand(ab) for ab in range(4)]
        layer_product(1, [(512, 576), (704, COEF0)], operands)
        layer_rims(1, range(8, 9))
        for ab in range(4):
            send_rim[turn, ab] = zl[1, ab, 512:576].astype(BF16)
        rim_copy = remote(send_rim.at[turn], b_rim.at[turn], 11 + turn, right)
        if turn == 1:
            bottom_planes(0, range(1, 8))
            before_rim.wait_recv()
            bottom_planes(0, range(0, 1))
            build_rim(0)
            bottom_product()
        layer_product(1, [(0, 512), (MAIN, 704)], operands)
        layer_rims(1, range(0, 8))
        bottom_planes_partly(turn)
        plane_copy = remote(send_plane.at[turn + 1], a_plane.at[turn + 1], turn + 1, left)
        build_rim(0)
        held_copy = send_held_of(turn + 1)
        top_planes(turn)
        if turn == 1:
            early = pltpu.make_async_copy(out_v.at[9:16], out_hbm.at[9:16], store_sem.at[0])
            early.start()
        if turn == 0:
            take_set_up(setting)
        parts, extra = finish_plane(turn + 1)
        coef_copy.wait_recv()
        spread_coef = dot(both[:COEF0, 0:CH], b_coef[turn])
        for ab in range(4):
            zl[0, ab, 0:COEF0] = spread_coef * chosen(upper_col, ab)
        layer_rims(0, range(9))
        if turn == 0:
            bottom_planes(turn, range(8, 9))
            before_rim = rim_copy
        else:
            bottom_planes(turn, range(1, 9))
            late = pltpu.make_async_copy(out_v.at[1:9], out_hbm.at[1:9], store_sem.at[1])
            late.start()
    rim_copy.wait_recv()
    bottom_planes(1, range(0, 1))

    first = pltpu.make_async_copy(out_v.at[0:1], out_hbm.at[0:1], store_sem.at[3])
    first.start()
    coef_v[0] = top_coef(2, plane_copy, held_copy, parts, extra)
    last = pltpu.make_async_copy(coef_v, coef_hbm, store_sem.at[2])
    last.start()
    for copy in copies:
        copy.wait_send()
    early.wait()
    late.wait()
    first.wait()
    last.wait()


def hand_on(field, coef, field_out, coef_out, held, coef_held, sem):
    pairs = [(coef, coef_held, coef_out)]
    for part in range(4):
        planes = pl.ds(4 * part, 4)
        pairs.append((field.at[planes], held.at[planes], field_out.at[planes]))
    inward = [pltpu.make_async_copy(x, y, sem.at[k]) for k, (x, y, _) in enumerate(pairs)]
    outward = [pltpu.make_async_copy(y, z, sem.at[5 + k]) for k, (_, y, z) in enumerate(pairs)]
    for copy in inward:
        copy.start()
    for first, second in zip(inward, outward):
        first.wait()
        second.start()
    for copy in outward:
        copy.wait()


def per_device(*arrays):
    arrays = list(arrays)
    wave_in = arrays[0]
    arrays[5] = jnp.swapaxes(arrays[5], 1, 2)
    arrays[6] = jnp.swapaxes(arrays[6], 1, 2)
    any_space = pl.BlockSpec(memory_space=pl.ANY)
    results = pl.pallas_call(
        kernel,
        out_shape=(
            jax.ShapeDtypeStruct(wave_in.shape, BF16),
            jax.ShapeDtypeStruct((1, CH, 128), F32),
        ),
        in_specs=[any_space] * 8 + [pl.BlockSpec(memory_space=pltpu.SMEM)] * 3,
        out_specs=(any_space, any_space),
        scratch_shapes=[
            pltpu.VMEM((16, 16, 16, 128), BF16),
            pltpu.VMEM((16, 256), F32),
            pltpu.VMEM((16, 256), F32),
            pltpu.VMEM((NODES, NODES), BF16),
            pltpu.VMEM((1, CH, NODES), BF16),
            pltpu.VMEM((1, CH, NODES), BF16),
            pltpu.VMEM((2, 2, 2), F32),
            pltpu.VMEM((1, CH), F32),
            pltpu.VMEM((16, 16, 16, 128), BF16),
            pltpu.VMEM((1, CH, 128), F32),
            pltpu.VMEM((DEPTH, NODES), BF16),
            pltpu.VMEM((DEPTH, DEPTH), BF16),
            pltpu.VMEM((DEPTH, 128), BF16),
            pltpu.VMEM((2 * CH, DEPTH), BF16),
            pltpu.VMEM((4, 1024, 128), F32),
            pltpu.VMEM((4, 1024, 128), F32),
            pltpu.VMEM((4, FACE, 128), F32),
            pltpu.VMEM((4, 1024, 128), BF16),
            pltpu.VMEM((4, 1088, 128), F32),
            pltpu.VMEM((2, 4, FACE, 128), BF16),
            pltpu.VMEM((2, 4, COEF0, 128), F32),
            pltpu.VMEM((4, 1024, 128), BF16),
            pltpu.VMEM((4, MAIN, 128), F32),
            pltpu.VMEM((4, 64, 128), BF16),
            pltpu.VMEM((4, 64, 128), F32),
            pltpu.VMEM((4, 96, 128), F32),
            pltpu.VMEM((256, CH), BF16),
            pltpu.VMEM((3, 4, 64, 128), BF16),
            pltpu.VMEM((3, CH, 128), F32),
            pltpu.VMEM((CH, 256), BF16),
            pltpu.VMEM((8, 256), F32),
            pltpu.VMEM((2, CH, 128), F32),
            pltpu.VMEM((2, 4, 64, 128), BF16),
            pltpu.VMEM((2, CH, 128), BF16),
            pltpu.VMEM((3, 4, 64, 128), BF16),
            pltpu.VMEM((3, CH, 128), F32),
            pltpu.VMEM((CH, 256), BF16),
            pltpu.VMEM((2, CH, 128), F32),
            pltpu.VMEM((2, 4, 64, 128), BF16),
            pltpu.VMEM((2, CH, 128), BF16),
            pltpu.SemaphoreType.DMA((9,)),
            pltpu.SemaphoreType.DMA((4,)),
            pltpu.SemaphoreType.DMA((13,)),
            pltpu.SemaphoreType.DMA((13,)),
        ],
        compiler_params=pltpu.CompilerParams(
            collective_id=0, has_side_effects=True, vmem_limit_bytes=63 * 1024 * 1024
        ),
    )(*arrays)
    return pl.pallas_call(
        hand_on,
        out_shape=(
            jax.ShapeDtypeStruct(wave_in.shape, BF16),
            jax.ShapeDtypeStruct((1, CH, 128), F32),
        ),
        in_specs=[any_space] * 2,
        out_specs=(any_space, any_space),
        scratch_shapes=[
            pltpu.VMEM((16, 16, 16, 128), BF16),
            pltpu.VMEM((1, CH, 128), F32),
            pltpu.SemaphoreType.DMA((10,)),
        ],
    )(*results)


def solution(mesh):
    in_specs = (
        P("space", None, None, "band"),
        P("space", None),
        P("space", None),
        P("space", None, None),
        P(),
        P("space", None, None),
        P("space", None, None),
        P("space", None),
        P("space"),
        P("space"),
        P("space"),
    )
    out_specs = (P("space", None, None, "band"), P("space", None, "band"))
    return jax.shard_map(
        per_device, mesh=mesh, in_specs=in_specs, out_specs=out_specs, check_vma=False
    )
```

```python
import functools

import jax
import jax.numpy as jnp
from jax import lax
from jax.experimental import pallas as pl
from jax.experimental.pallas import tpu as pltpu
from jax.sharding import PartitionSpec as P

MESH = pl.DeviceIdType.MESH
F32 = jnp.float32
BF16 = jnp.bfloat16

DEPTH = 768
MAIN = 576
FACE = 192
EDGE0 = 720
COEF0 = 736
NODES = 729
CH = 32


def node_selector():
    row = lax.broadcasted_iota(jnp.int32, (DEPTH, 128), 0)
    face = row - MAIN
    edge = row - EDGE0
    spot = jnp.bitwise_and(face, 15)
    old_main = (row >> 6) * 81 + jnp.bitwise_and(row >> 3, 7) * 9 + jnp.bitwise_and(row, 7)
    old_face = (face >> 4) * 81 + jnp.where(spot < 8, 72 + spot, (spot - 8) * 9 + 8)
    old_edge = jnp.where(edge < 9, edge * 81 + 80, -1)
    old = jnp.where(row < MAIN, old_main, jnp.where(row < EDGE0, old_face, old_edge))
    column = lax.broadcasted_iota(jnp.int32, (DEPTH, 128), 1)
    pieces = []
    for part in range(6):
        pieces.append((old == column + part * 128).astype(F32).astype(BF16))
    return jnp.concatenate(pieces, axis=1)[:, :NODES]


def dot(left, right):
    return jnp.dot(left, right, preferred_element_type=F32)


def dot_turned(left, right):
    return lax.dot_general(left, right, (((1,), (1,)), ((), ())), preferred_element_type=F32)


def kernel(
    wave_hbm, mass_hbm, pot_hbm, scale_hbm, stiff_hbm, lower_hbm, upper_hbm, kb_hbm, atom_ref, count_ref, next_ref,
    out_hbm, coef_hbm,
    wave, mass, pot, stiff, lower, upper, scale, kb, out_v, coef_v,
    sel, kp, both, both_t, massb, potb, mrim, wv, wf, rim, zl, stepv, pf, plane16, mass16, ez, e0,
    a_plane, a_held, a_edge, a_mass, a_gram, b_rim, b_coef,
    send_plane, send_held, send_edge, send_gram, send_rim, send_coef,
    load_sem, store_sem, send_sem, recv_sem,
):
    me = lax.axis_index("space")
    n = lax.axis_size("space")
    right, left = lax.rem(me + 1, n), lax.rem(me + n - 1, n)
    share = (1.0 / 6.0, 2.0 / 6.0)
    atom_col, count, upper_col = atom_ref[0], count_ref[0], next_ref[0]

    barrier = pltpu.get_barrier_semaphore()
    for neighbour in (left, right):
        pl.semaphore_signal(barrier, inc=1, device_id={"space": neighbour}, device_id_type=MESH)

    loads = []
    for slot, (source, target) in enumerate(
        [
            (mass_hbm, mass),
            (upper_hbm, upper),
            (lower_hbm, lower),
            (wave_hbm.at[0:9], wave.at[0:9]),
            (stiff_hbm, stiff),
            (wave_hbm.at[9:16], wave.at[9:16]),
            (pot_hbm, pot),
            (scale_hbm, scale),
            (kb_hbm, kb),
        ]
    ):
        copy = pltpu.make_async_copy(source, target, load_sem.at[slot])
        copy.start()
        loads.append(copy)

    copies = []

    def remote(source, target, slot, neighbour):
        copy = pltpu.make_async_remote_copy(
            src_ref=source,
            dst_ref=target,
            send_sem=send_sem.at[slot],
            recv_sem=recv_sem.at[slot],
            device_id={"space": neighbour},
            device_id_type=MESH,
        )
        copy.start()
        copies.append(copy)
        return copy

    sel[...] = node_selector()
    for layer in range(2):
        for ab in range(4):
            rim[layer, ab, 160:192] = jnp.zeros((32, 128), BF16)

    def spread(turned, target, planes):
        turned = turned.reshape(2, 8, 2, 8, turned.shape[-1])
        for p in planes:
            for a in range(2):
                for b in range(2):
                    block = turned[a, :, b, :, p : p + 1]
                    target[2 * a + b, p * 64 : p * 64 + 64] = jnp.broadcast_to(block, (8, 8, 128)).reshape(64, 128)

    def wave_block(p, a):
        both_b = wave[p, 8 * a : 8 * a + 8].astype(F32)
        return [both_b[:, 8 * b : 8 * b + 8].reshape(64, 128) for b in range(2)]

    def put_field(ab, p, value):
        rounded = value.astype(BF16)
        wv[ab, p * 64 : p * 64 + 64] = rounded
        wf[ab, p * 64 : p * 64 + 64] = rounded.astype(F32)

    def gather_rim(source, base, put):
        for a in range(2):
            for b in range(2):
                ab = 2 * a + b
                for i in range(9):
                    at = base + i * 64
                    j_face = source[2 * (1 - a) + b, at : at + 8]
                    l_face = source[2 * a + (1 - b), pl.ds(at, 8, stride=8)]
                    put(ab, i * 16, jnp.concatenate([j_face, l_face], axis=0))
                other = 2 * (1 - a) + (1 - b)
                edge = source[other, pl.ds(base, 8, stride=64)]
                last = source[other, base + 512 : base + 520]
                put(ab, 144, jnp.concatenate([edge, last], axis=0))

    def build_rim(layer):
        def put(ab, row, value):
            rim[layer, ab, row : row + 16] = value.astype(BF16)

        gather_rim(wf, 512 * layer, put)

    def bottom_operand(ab):
        return jnp.concatenate([wv[ab, 0:MAIN], rim[0, ab]], axis=0)

    def top_operand(ab):
        return jnp.concatenate([wv[ab, 512:1024], plane16[ab], rim[1, ab]], axis=0)

    loads[0].wait()
    spread(jnp.transpose(mass[...]), massb, range(16))
    loads[1].wait()
    loads[2].wait()
    turned = dot_turned(jnp.concatenate([upper[0], lower[0]], axis=0), sel[...])
    both_t[...] = turned.astype(BF16)
    loads[3].wait()

    def start_field(planes):
        for p in planes:
            for a in range(2):
                for b, block in enumerate(wave_block(p, a)):
                    put_field(2 * a + b, p, massb[2 * a + b, p * 64 : p * 64 + 64] * block)

    def send_held_of(turn):
        send_held[turn] = dot(both_t[0:CH], bottom_operand(upper_col))
        return remote(send_held.at[turn], a_held.at[turn], 3 + turn, left)

    start_field(range(0, 1))
    for ab in range(4):
        send_plane[0, ab] = wv[ab, 0:64]
    start_field(range(1, 9))
    build_rim(0)
    send_held[0] = dot(both_t[0:CH], bottom_operand(upper_col))
    pl.semaphore_wait(barrier, 2)
    plane_copy = remote(send_plane.at[0], a_plane.at[0], 0, left)
    held_copy = remote(send_held.at[0], a_held.at[0], 3, left)
    both[...] = jnp.transpose(jnp.concatenate([turned, jnp.zeros((64, DEPTH), F32)], axis=0)).astype(BF16)
    loads[4].wait()
    spans = [(0, 256, slice(0, 384)), (256, 512, slice(256, NODES)), (512, DEPTH, slice(0, NODES))]
    half = jnp.concatenate([dot(sel[low:high, old], stiff[old]) for low, high, old in spans], axis=0).astype(BF16)
    for low, high, old in spans:
        kp[:, low:high] = dot_turned(half[:, old], sel[low:high, old]).astype(BF16)
    kp[:, COEF0:] = both[:, CH : 2 * CH]
    for slot in (5, 6, 7, 8):
        loads[slot].wait()
    start_field(range(9, 16))
    spread(jnp.transpose(pot[...]), potb, range(16))

    channel = lax.broadcasted_iota(jnp.int32, (CH, CH), 1)
    square = lax.broadcasted_iota(jnp.int32, (CH, CH), 0) == channel
    live = jnp.logical_and(square, channel < count)
    weight = jnp.sum(jnp.where(live, jnp.broadcast_to(kb[...], (CH, CH)), 0.0), axis=1, keepdims=True)

    def scale_of(layer, ab, rows):
        return jnp.broadcast_to(scale[layer, ab // 2 : ab // 2 + 1, ab % 2 : ab % 2 + 1], (rows, 128))

    def chosen(column, ab):
        return jnp.where(column == ab, 1.0, 0.0)

    def layer_product(layer, rows, operands):
        for pair in range(2):
            wide = jnp.concatenate(operands[2 * pair : 2 * pair + 2], axis=1)
            for low, high in rows:
                product = dot(kp[low:high], wide)
                for k in range(2):
                    ab = 2 * pair + k
                    zl[layer, ab, low:high] = product[:, 128 * k : 128 * k + 128] * scale_of(layer, ab, high - low)

    def add_rims(target, planes, face, edge_row):
        for i in planes:
            for a in range(2):
                for b in range(2):
                    ab = 2 * a + b
                    j_at, l_at, e_at = 2 * (1 - a) + b, 2 * a + (1 - b), 2 * (1 - a) + (1 - b)
                    j_face = target[ab, face + i * 16 : face + i * 16 + 8]
                    l_face = target[ab, face + i * 16 + 8 : face + i * 16 + 16]
                    edge = target[ab, edge_row + i : edge_row + i + 1]
                    target[j_at, i * 64 : i * 64 + 8] = target[j_at, i * 64 : i * 64 + 8] + j_face
                    rows = pl.ds(i * 64, 8, stride=8)
                    target[l_at, rows] = target[l_at, rows] + l_face
                    target[e_at, i * 64 : i * 64 + 1] = target[e_at, i * 64 : i * 64 + 1] + edge

    def layer_rims(layer, planes):
        add_rims(zl.at[layer], planes, MAIN, EDGE0)

    def set_up():
        for ab in range(4):
            part = chosen(upper_col, ab)
            ez[ab, 0:64] = both[0:64].astype(F32) * part
            ez[ab, 64:80] = both[MAIN : MAIN + 16].astype(F32) * part
            ez[ab, 80:96] = both[EDGE0 : EDGE0 + 16].astype(F32) * part
        add_rims(ez, range(1), 64, 80)
        placed = jnp.transpose(jnp.concatenate([ez[ab, 0:64] for ab in range(4)], axis=0))
        send_edge[...] = placed[0:CH].astype(BF16)
        sent = [remote(send_edge, a_edge, 6, left), remote(mass.at[0:8], a_mass, 7, left)]

        def put(ab, row, value):
            mrim[ab, row : row + 16] = value

        for ab in range(4):
            mrim[ab, 160:192] = jnp.zeros((32, 128), F32)
        gather_rim(massb, 0, put)
        at = upper_col
        node_mass = jnp.concatenate([massb[at, 0:MAIN], mrim[at]], axis=0)
        wide = both[...].astype(F32) * node_mass
        send_gram[0] = dot(both_t[0:CH], (wide * node_mass).astype(BF16)) * share[0]
        send_gram[1] = dot(both_t[0:CH], wide.astype(BF16)) * share[1]
        sent.append(remote(send_gram, a_gram, 8, left))
        return sent

    def take_set_up(sent):
        for copy in sent:
            copy.wait_recv()
        wide = jnp.concatenate([a_edge[...].astype(F32), jnp.zeros((128 - CH, 256), F32)], axis=0)
        e0[...] = jnp.transpose(wide)[:, 0:CH].astype(BF16)
        spread(jnp.transpose(a_mass[...]), mass16, range(1))

    def finish_plane(turn):
        before = turn - 1
        coef = send_coef[before]
        placed = dot(e0[...], coef)
        shares = []
        parts = []
        for ab in range(4):
            edge_sum = send_rim[before, ab].astype(F32)
            amount = mass16[ab] * share[before]
            parts.append(amount * (edge_sum + placed[64 * ab : 64 * ab + 64]))
            shares.append((amount * edge_sum * mass16[ab] if turn == 1 else amount * edge_sum).astype(BF16))
        held = dot(a_edge[...], jnp.concatenate(shares, axis=0))
        held = held + jnp.dot(
            a_gram[before, :, 0:CH], coef.astype(F32), preferred_element_type=F32, precision=lax.Precision.HIGHEST
        )
        return parts, held

    def top_coef(turn, plane_copy, held_copy, parts, extra):
        plane_copy.wait_recv()
        for ab in range(4):
            value = a_plane[turn, ab].astype(F32)
            if turn > 0:
                value = value + parts[ab]
            if turn == 1:
                value = mass16[ab] * value.astype(BF16).astype(F32)
            value = value.astype(BF16)
            plane16[ab] = value
            wf[ab, 1024:1088] = value.astype(F32)
        build_rim(1)
        own = dot(both_t[CH : 2 * CH], top_operand(atom_col))
        held_copy.wait_recv()
        own = own + a_held[turn]
        return own if turn == 0 else own + extra

    def combine(turn, p, ab, total, wave_part):
        rows = slice(p * 64, p * 64 + 64)
        image = massb[ab, rows] * (total + potb[ab, rows] * wf[ab, rows])
        if turn == 0:
            return (image - wave_part) * share[0]
        return share[1] * (image - stepv[ab, rows].astype(F32)) - wave_part

    def keep(turn, p, a, values):
        if turn == 0:
            for b in range(2):
                ab = 2 * a + b
                step = values[b].astype(BF16)
                stepv[ab, p * 64 : p * 64 + 64] = step
                put_field(ab, p, massb[ab, p * 64 : p * 64 + 64] * step.astype(F32))
            return
        if p >= 8:
            for b in range(2):
                put_field(2 * a + b, p, values[b])
        pieces = [value.reshape(8, 8, 128) for value in values]
        out_v[p, 8 * a : 8 * a + 8] = jnp.concatenate(pieces, axis=1).astype(BF16)

    def top_planes(turn):
        for p in range(9, 16):
            for a in range(2):
                waves = wave_block(p, a)
                values = []
                for b in range(2):
                    ab = 2 * a + b
                    total = zl[1, ab, (p - 8) * 64 : (p - 8) * 64 + 64]
                    values.append(combine(turn, p, ab, total, waves[b]))
                keep(turn, p, a, values)

    def bottom_planes_partly(turn):
        for p in range(9):
            for a in range(2):
                waves = wave_block(p, a)
                for b in range(2):
                    ab = 2 * a + b
                    rows = slice(p * 64, p * 64 + 64)
                    total = zl[0, ab, rows]
                    if p == 8:
                        total = total + zl[1, ab, 0:64]
                    value = combine(turn, p, ab, total, waves[b])
                    pf[ab, rows] = value
                    if p == 0:
                        send_plane[turn + 1, ab] = value.astype(BF16)
                    put_field(ab, p, massb[ab, rows] * value if turn == 0 else value)

    def bottom_planes(turn, planes):
        for p in planes:
            for a in range(2):
                values = []
                for b in range(2):
                    ab = 2 * a + b
                    rows = slice(p * 64, p * 64 + 64)
                    extra = zl[0, ab, rows]
                    if p == 0:
                        extra = extra + b_rim[turn, ab].astype(F32)
                    values.append(pf[ab, rows] + massb[ab, rows] * share[turn] * extra)
                keep(turn, p, a, values)

    def bottom_product():
        layer_product(0, [(0, COEF0)], [bottom_operand(ab) for ab in range(4)])
        layer_rims(0, range(9))

    parts, extra = None, None
    for turn in range(2):
        if turn == 0:
            bottom_product()
            setting = set_up()
        total = top_coef(turn, plane_copy, held_copy, parts, extra) * weight
        send_coef[turn] = total.astype(BF16)
        coef_copy = remote(send_coef.at[turn], b_coef.at[turn], 9 + turn, right)
        for ab in range(4):
            part = (total / scale_of(1, ab, CH)) * chosen(atom_col, ab)
            rim[1, ab, 160:192] = part.astype(BF16)
        operands = [top_operand(ab) for ab in range(4)]
        layer_product(1, [(512, 576), (704, COEF0)], operands)
        layer_rims(1, range(8, 9))
        for ab in range(4):
            send_rim[turn, ab] = zl[1, ab, 512:576].astype(BF16)
        rim_copy = remote(send_rim.at[turn], b_rim.at[turn], 11 + turn, right)
        if turn == 1:
            bottom_product()
        layer_product(1, [(0, 512), (MAIN, 704)], operands)
        layer_rims(1, range(0, 8))
        bottom_planes_partly(turn)
        plane_copy = remote(send_plane.at[turn + 1], a_plane.at[turn + 1], turn + 1, left)
        build_rim(0)
        held_copy = send_held_of(turn + 1)
        top_planes(turn)
        if turn == 1:
            early = pltpu.make_async_copy(out_v.at[9:16], out_hbm.at[9:16], store_sem.at[0])
            early.start()
        if turn == 0:
            take_set_up(setting)
        parts, extra = finish_plane(turn + 1)
        coef_copy.wait_recv()
        spread_coef = dot(both[:COEF0, 0:CH], b_coef[turn])
        for ab in range(4):
            zl[0, ab, 0:COEF0] = spread_coef * chosen(upper_col, ab)
        layer_rims(0, range(9))
        bottom_planes(turn, range(8, 9))
        if turn == 1:
            coef_v[0] = top_coef(2, plane_copy, held_copy, parts, extra)
            last = pltpu.make_async_copy(coef_v, coef_hbm, store_sem.at[2])
            last.start()
        bottom_planes(turn, range(1, 8))
        if turn == 1:
            late = pltpu.make_async_copy(out_v.at[1:9], out_hbm.at[1:9], store_sem.at[1])
            late.start()
        rim_copy.wait_recv()
        bottom_planes(turn, range(0, 1))
        if turn == 0:
            build_rim(0)

    first = pltpu.make_async_copy(out_v.at[0:1], out_hbm.at[0:1], store_sem.at[3])
    first.start()
    for copy in copies:
        copy.wait_send()
    early.wait()
    late.wait()
    first.wait()
    last.wait()


def hand_on(field, coef, field_out, coef_out, held, coef_held, sem):
    pairs = [(coef, coef_held, coef_out)]
    for part in range(8):
        planes = pl.ds(2 * part, 2)
        pairs.append((field.at[planes], held.at[planes], field_out.at[planes]))
    inward = [pltpu.make_async_copy(x, y, sem.at[k]) for k, (x, y, _) in enumerate(pairs)]
    outward = [pltpu.make_async_copy(y, z, sem.at[9 + k]) for k, (_, y, z) in enumerate(pairs)]
    for copy in inward:
        copy.start()
    for first, second in zip(inward, outward):
        first.wait()
        second.start()
    for copy in outward:
        copy.wait()


def per_device(*arrays):
    arrays = list(arrays)
    wave_in = arrays[0]
    arrays[5] = jnp.swapaxes(arrays[5], 1, 2)
    arrays[6] = jnp.swapaxes(arrays[6], 1, 2)
    any_space = pl.BlockSpec(memory_space=pl.ANY)
    results = pl.pallas_call(
        kernel,
        out_shape=(
            jax.ShapeDtypeStruct(wave_in.shape, BF16),
            jax.ShapeDtypeStruct((1, CH, 128), F32),
        ),
        in_specs=[any_space] * 8 + [pl.BlockSpec(memory_space=pltpu.SMEM)] * 3,
        out_specs=(any_space, any_space),
        scratch_shapes=[
            pltpu.VMEM((16, 16, 16, 128), BF16),
            pltpu.VMEM((16, 256), F32),
            pltpu.VMEM((16, 256), F32),
            pltpu.VMEM((NODES, NODES), BF16),
            pltpu.VMEM((1, CH, NODES), BF16),
            pltpu.VMEM((1, CH, NODES), BF16),
            pltpu.VMEM((2, 2, 2), F32),
            pltpu.VMEM((1, CH), F32),
            pltpu.VMEM((16, 16, 16, 128), BF16),
            pltpu.VMEM((1, CH, 128), F32),
            pltpu.VMEM((DEPTH, NODES), BF16),
            pltpu.VMEM((DEPTH, DEPTH), BF16),
            pltpu.VMEM((DEPTH, 128), BF16),
            pltpu.VMEM((2 * CH, DEPTH), BF16),
            pltpu.VMEM((4, 1024, 128), F32),
            pltpu.VMEM((4, 1024, 128), F32),
            pltpu.VMEM((4, FACE, 128), F32),
            pltpu.VMEM((4, 1024, 128), BF16),
            pltpu.VMEM((4, 1088, 128), F32),
            pltpu.VMEM((2, 4, FACE, 128), BF16),
            pltpu.VMEM((2, 4, COEF0, 128), F32),
            pltpu.VMEM((4, 1024, 128), BF16),
            pltpu.VMEM((4, MAIN, 128), F32),
            pltpu.VMEM((4, 64, 128), BF16),
            pltpu.VMEM((4, 64, 128), F32),
            pltpu.VMEM((4, 96, 128), F32),
            pltpu.VMEM((256, CH), BF16),
            pltpu.VMEM((3, 4, 64, 128), BF16),
            pltpu.VMEM((3, CH, 128), F32),
            pltpu.VMEM((CH, 256), BF16),
            pltpu.VMEM((8, 256), F32),
            pltpu.VMEM((2, CH, 128), F32),
            pltpu.VMEM((2, 4, 64, 128), BF16),
            pltpu.VMEM((2, CH, 128), BF16),
            pltpu.VMEM((3, 4, 64, 128), BF16),
            pltpu.VMEM((3, CH, 128), F32),
            pltpu.VMEM((CH, 256), BF16),
            pltpu.VMEM((2, CH, 128), F32),
            pltpu.VMEM((2, 4, 64, 128), BF16),
            pltpu.VMEM((2, CH, 128), BF16),
            pltpu.SemaphoreType.DMA((9,)),
            pltpu.SemaphoreType.DMA((4,)),
            pltpu.SemaphoreType.DMA((13,)),
            pltpu.SemaphoreType.DMA((13,)),
        ],
        compiler_params=pltpu.CompilerParams(
            collective_id=0, has_side_effects=True, vmem_limit_bytes=63 * 1024 * 1024
        ),
    )(*arrays)
    return pl.pallas_call(
        hand_on,
        out_shape=(
            jax.ShapeDtypeStruct(wave_in.shape, BF16),
            jax.ShapeDtypeStruct((1, CH, 128), F32),
        ),
        in_specs=[any_space] * 2,
        out_specs=(any_space, any_space),
        scratch_shapes=[
            pltpu.VMEM((16, 16, 16, 128), BF16),
            pltpu.VMEM((1, CH, 128), F32),
            pltpu.SemaphoreType.DMA((18,)),
        ],
    )(*results)


def solution(mesh):
    in_specs = (
        P("space", None, None, "band"),
        P("space", None),
        P("space", None),
        P("space", None, None),
        P(),
        P("space", None, None),
        P("space", None, None),
        P("space", None),
        P("space"),
        P("space"),
        P("space"),
    )
    out_specs = (P("space", None, None, "band"), P("space", None, "band"))
    return jax.shard_map(
        per_device, mesh=mesh, in_specs=in_specs, out_specs=out_specs, check_vma=False
    )
```
